32 devices in a mesh: space: 8 (over z, x), probe: 4 (over y, core).
Axes of the slice: x: 2, y: 2, z: 4, core: 2. Of those that a mesh axis runs over, the one named last changes fastest.
Arguments:
- probes: float32 [128, 16, 128, 128], P('probe', 'space'), may hold values from -20 to 20, as said below
- winds: float32 [4, 3, 16, 128, 128], P(None, None, 'space'), may hold values from -0.12 to 0.12
- wind_step: int32 [16], P('space'), may hold values from 0 to 3
- obs_weight: float32 [16, 128, 128], P('space'), may hold values from 0.5 to 6, as said below
- prior_weight: float32 [16, 128, 128], P('space'), may hold values from 0.2 to 3, as said below
Outputs:
- basis_out: float32 [128, 16, 128, 128], P(None, 'space', 'probe')
- r_factor: float32 [128, 128], replicated
The draws below stay inside these ranges and needn't reach their ends.
Inputs may be any that keep to these rules, and one draw needn't show every extreme that they name: `probes`: probe vectors of unlike scales with parts in common between them. `obs_weight`: positive. `prior_weight`: positive.
All inputs are finite; a program needn't handle non-finite values.
Results may differ from the reference program's by a relative error of at most 0.00011.
Values sent between devices are 32-bit elements; how exact they have to be, the bound alone decides.
A program may use at most 128 MiB of HBM per device.

```python
import math
import jax
import jax.numpy as jnp
from jax import lax

K = 128
NY = 128
NZ = 128
STEPS = 4
NX = 16
CELLS = 262144


def ramp_factor(exponent):
    position = jnp.arange(NX, dtype=jnp.float32) / max(NX - 1, 1)
    return (3.0 ** (exponent * position))[:, None, None]


def draw_probes(key, part):
    key = jax.random.fold_in(key, 11)
    noise_key = jax.random.fold_in(key, 1)
    scale_key = jax.random.fold_in(key, 2)
    noise_all = jax.random.truncated_normal(noise_key, -4.0, 4.0, (K, NX, NY, NZ), jnp.float32)
    scales = jnp.exp(jax.random.uniform(scale_key, (K,), jnp.float32, math.log(0.3), math.log(3.0)))
    mixed_all = noise_all + 0.6 * jnp.roll(noise_all, 1, axis=0)
    return mixed_all * scales[:, None, None, None]


def draw_obs_weight(key, part):
    key = jax.random.fold_in(key, 21)
    base_field = jnp.exp(jax.random.uniform(key, (NX, NY, NZ), jnp.float32, math.log(0.5), math.log(2.0)))
    return base_field * ramp_factor(0.5)


def draw_prior_weight(key, part):
    key = jax.random.fold_in(key, 31)
    base_field = jnp.exp(jax.random.uniform(key, (NX, NY, NZ), jnp.float32, math.log(0.2), math.log(1.0)))
    return base_field * ramp_factor(0.5)


def touch_ends(values, own_key, least, largest):
    extent = values.shape
    index_at = [jax.random.randint(jax.random.fold_in(own_key, axis), (), 0, extent[axis]) for axis in range(len(extent))]
    values = values.at[tuple(index_at)].set(least)
    longest = extent.index(max(extent))
    index_at[longest] = (index_at[longest] + 1) % extent[longest]
    return values.at[tuple(index_at)].set(largest)


def shard_levels(stream_key, extent, shards, smallest, high):
    def one(axis_at, parts):
        heights = jax.random.uniform(jax.random.fold_in(jax.random.fold_in(stream_key, 6), axis_at), (parts,), jnp.float32, smallest / len(shards), high / len(shards))
        return jnp.repeat(jnp.exp(heights), extent[axis_at] // parts).reshape((-1,) + (1,) * (len(extent) - axis_at - 1))

    factor_of = one(*shards[0])
    for cut in shards[1:]:
        factor_of = factor_of * one(*cut)
    return factor_of


def setup_inputs(seed: int = 0) -> dict:
    keys = jax.random.split(jax.random.key(seed), 6)
    probes = draw_probes(jax.random.fold_in(keys[5], 71), 0)
    winds = jnp.clip(jax.random.uniform(keys[1], (STEPS, 3, NX, NY, NZ), jnp.float32, -0.12, 0.12) * shard_levels(keys[1], (STEPS, 3, NX, NY, NZ), ((2, 8),), -0.4, 0.0), -0.12, 0.12)
    wind_step = touch_ends(jax.random.randint(keys[2], (NX,), 0, STEPS), jax.random.fold_in(keys[2], 1), 0, STEPS - 1).astype(jnp.int32)
    obs_weight = draw_obs_weight(jax.random.fold_in(keys[5], 71), 0)
    prior_weight = draw_prior_weight(jax.random.fold_in(keys[5], 71), 0)
    return dict(probes=probes, winds=winds, wind_step=wind_step, obs_weight=obs_weight, prior_weight=prior_weight)


diffusion = 0.1

def neighbours(state_in, axis_dim):
    pad_width = [(0, 0)] * state_in.ndim
    pad_width[axis_dim] = (1, 1)
    padded = jnp.pad(state_in, pad_width)
    length_dim = state_in.shape[axis_dim]
    next_cells = lax.slice_in_dim(padded, 2, length_dim + 2, axis=axis_dim)
    prev_cells = lax.slice_in_dim(padded, 0, length_dim, axis=axis_dim)
    return (next_cells, prev_cells)

def tangent(state_in, wind_now):
    result_sum = state_in
    for axis_dim in range(3):
        next_cells, prev_cells = neighbours(state_in, axis_dim + 1)
        speed_pos = jnp.maximum(wind_now[axis_dim], 0.0)
        speed_neg = jnp.minimum(wind_now[axis_dim], 0.0)
        result_sum = result_sum - speed_pos * (state_in - prev_cells) - speed_neg * (next_cells - state_in)
        result_sum = result_sum + diffusion * (next_cells - 2.0 * state_in + prev_cells)
    return result_sum

def adjoint(state_in, wind_now):
    result_sum = state_in
    for axis_dim in range(3):
        next_cells, prev_cells = neighbours(state_in, axis_dim + 1)
        flux_pos = jnp.maximum(wind_now[axis_dim], 0.0) * state_in
        flux_neg = jnp.minimum(wind_now[axis_dim], 0.0) * state_in
        pos_next = neighbours(flux_pos, axis_dim + 1)[0]
        neg_prev = neighbours(flux_neg, axis_dim + 1)[1]
        result_sum = result_sum - flux_pos + pos_next + flux_neg - neg_prev
        result_sum = result_sum + diffusion * (next_cells - 2.0 * state_in + prev_cells)
    return result_sum

def select_wind(winds, wind_step):
    levels = jnp.arange(winds.shape[0], dtype=jnp.int32)
    picked = levels[:, None] == wind_step.astype(jnp.int32)[None, :]
    return lax.optimization_barrier(jnp.sum(jnp.where(picked[:, None, :, None, None], winds, jnp.zeros_like(winds)), axis=0))

def reference(probes, winds, wind_step, obs_weight, prior_weight):
    wind_now = select_wind(winds, wind_step)

    def hessian(probe_block):
        forward = tangent(probe_block, wind_now)
        weighted = obs_weight * forward
        return adjoint(weighted, wind_now) + prior_weight * probe_block
    grouped = probes.reshape(K // 8, 8, NX, NY, NZ)
    hess_image = lax.map(hessian, grouped).reshape(K, NX * NY * NZ)
    gram_matrix = lax.dot_general(hess_image.astype(jnp.float32), hess_image.astype(jnp.float32), (((1,), (1,)), ((), ())), precision=lax.Precision.HIGHEST, preferred_element_type=jnp.float32)
    low_factor = jnp.linalg.cholesky(gram_matrix)
    solved = jax.scipy.linalg.solve_triangular(low_factor, hess_image, lower=True)
    norm_scale = math.sqrt(CELLS)
    basis_out = (solved * norm_scale).reshape(K, NX, NY, NZ)
    r_factor = low_factor.T / norm_scale
    return (basis_out, r_factor)
```

```python
import functools
import math

import jax
import jax.numpy as jnp
from jax import lax
from jax.experimental import pallas as pl
from jax.experimental.pallas import tpu as pltpu
from jax.sharding import PartitionSpec as P

diffusion = 0.1
MESH = pl.DeviceIdType.MESH
highest = lax.Precision.HIGHEST


def select_wind(winds, wind_step):
    levels = jnp.arange(winds.shape[0], dtype=jnp.int32)
    picked = levels[:, None] == wind_step[None, :]
    return jnp.sum(jnp.where(picked[:, None, :, None, None], winds, jnp.zeros_like(winds)), axis=0)


def exchange_kernel(
    n_space, n_probe, chunks, window,
    probes_ref, fields_ref, y_out, gram_out,
    field, fwd_state, coef, weighted, image, rows_ref, gram_part, reduce_buf, group_buf, total,
    own_sem, x_send, x_recv, zd_send, zf_send, lo_recv, hi_recv,
    f_own, f_xs, f_xr, f_zds, f_zfs, f_lor, f_hir,
    a_send, a_recv, a_own, r_send, r_recv, g_send, g_recv, t_send, t_recv, y_sem,
):
    space = lax.axis_index("space")
    probe = lax.axis_index("probe")
    side = lax.rem(space, 2)
    partner = space + 1 - 2 * side
    group = lax.div(space, 2)
    n_group = n_space // 2
    base = space - side
    n_peer = 2 * n_probe
    mine = side * n_probe + probe
    half = probes_ref.shape[0] // 2
    per = half // chunks
    ny, nz = probes_ref.shape[2], probes_ref.shape[3]
    band = ny // n_probe
    below, above = space - 2, space + 2
    has_lo, has_hi = group > 0, group < n_group - 1

    def peer(step):
        other = lax.rem(mine + step, n_peer)
        return other, lax.div(other, n_probe), lax.rem(other, n_probe)

    def sister(step):
        other = lax.rem(group + step, n_group)
        return other, 2 * other + side

    barrier = pltpu.get_barrier_semaphore()
    for step in range(1, n_peer):
        _, px, pp = peer(step)
        pl.semaphore_signal(barrier, inc=1, device_id=(base + px, pp), device_id_type=MESH)
    for step in range(1, n_group):
        pl.semaphore_signal(
            barrier, inc=1, device_id=(sister(step)[1], probe), device_id_type=MESH
        )
    pl.semaphore_wait(barrier, n_peer + n_group - 2)

    def remote(src, dst, send, recv, dev):
        return pltpu.make_async_remote_copy(
            src_ref=src, dst_ref=dst, send_sem=send, recv_sem=recv,
            device_id=dev, device_id_type=MESH,
        )

    own_plane = 2 + 2 * side
    got_plane = 4 - 2 * side

    own_f = pltpu.make_async_copy(fields_ref, field.at[pl.ds(1 + 2 * side, 2)], f_own)
    own_f.start()
    x_f = remote(fields_ref, field.at[pl.ds(1 + 2 * side, 2)], f_xs, f_xr, (partner, probe))
    x_f.start()

    def z_low(src, send):
        return remote(src, field.at[5, pl.ds(0, 4)], send, f_hir, (below, probe))

    def z_high(src, send):
        return remote(src, field.at[0, pl.ds(0, 4)], send, f_lor, (above, probe))

    direct_lo = (side == 0) & has_lo
    direct_hi = (side == 1) & has_hi
    relay_hi = (side == 0) & has_hi
    relay_lo = (side == 1) & has_lo

    @pl.when(direct_lo)
    def _():
        z_low(fields_ref.at[0, pl.ds(0, 4)], f_zds).start()

    @pl.when(direct_hi)
    def _():
        z_high(fields_ref.at[1, pl.ds(0, 4)], f_zds).start()

    def chunk_at(c):
        return pl.ds(c * per, per)

    def x_copy(c):
        return remote(
            probes_ref.at[pl.ds((1 - side) * half + c * per, per)],
            fwd_state.at[chunk_at(c), pl.ds(own_plane, 2)],
            x_send.at[c], x_recv.at[c], (partner, probe),
        )

    def own_copy(c):
        return pltpu.make_async_copy(
            probes_ref.at[pl.ds(side * half + c * per, per)],
            fwd_state.at[chunk_at(c), pl.ds(own_plane, 2)],
            own_sem.at[c],
        )

    def zd_src(c):
        return probes_ref.at[pl.ds(side * half + c * per, per)]

    def zf_src(c):
        return fwd_state.at[chunk_at(c), pl.ds(got_plane, 2)]

    def lo_copy(src, c, send):
        return remote(
            src, fwd_state.at[chunk_at(c), pl.ds(6, 2)], send.at[c], hi_recv.at[c], (below, probe)
        )

    def hi_copy(src, c, send):
        return remote(
            src, fwd_state.at[chunk_at(c), pl.ds(0, 2)], send.at[c], lo_recv.at[c], (above, probe)
        )

    def launch(c):
        x_copy(c).start()
        own_copy(c).start()

        @pl.when(direct_lo)
        def _():
            lo_copy(zd_src(c), c, zd_send).start()

        @pl.when(direct_hi)
        def _():
            hi_copy(zd_src(c), c, zd_send).start()

    for c in range(window):
        launch(c)

    @pl.when(jnp.logical_not(has_lo))
    def _():
        field[0] = jnp.zeros(field.shape[1:], jnp.float32)

        def clear(i, carry):
            fwd_state[i, pl.ds(0, 2)] = jnp.zeros((2, ny, nz), jnp.float32)
            return carry

        lax.fori_loop(0, half, clear, 0)

    @pl.when(jnp.logical_not(has_hi))
    def _():
        field[5] = jnp.zeros(field.shape[1:], jnp.float32)

        def clear(i, carry):
            fwd_state[i, pl.ds(6, 2)] = jnp.zeros((2, ny, nz), jnp.float32)
            return carry

        lax.fori_loop(0, half, clear, 0)

    x_f.wait_recv()

    @pl.when(relay_hi)
    def _():
        z_high(field.at[4, pl.ds(0, 4)], f_zfs).start()

    @pl.when(relay_lo)
    def _():
        z_low(field.at[1, pl.ds(0, 4)], f_zfs).start()

    own_f.wait()

    @pl.when(has_lo)
    def _():
        z_high(field.at[0, pl.ds(0, 4)], f_zfs).wait_recv()

    @pl.when(has_hi)
    def _():
        z_low(field.at[5, pl.ds(0, 4)], f_zfs).wait_recv()

    row_id = lax.broadcasted_iota(jnp.int32, (ny, nz), 0)
    col_id = lax.broadcasted_iota(jnp.int32, (ny, nz), 1)

    def make_coef(plane, carry):
        centre = jnp.full((ny, nz), 1.0 - 6.0 * diffusion, jnp.float32)
        for dim in range(3):
            speed = field[plane, dim]
            pos, neg = jnp.maximum(speed, 0.0), jnp.minimum(speed, 0.0)
            centre = centre - pos + neg
            up, down = pos + diffusion, diffusion - neg
            if dim == 1:
                up = jnp.where(row_id == 0, 0.0, up)
                down = jnp.where(row_id == ny - 1, 0.0, down)
            if dim == 2:
                up = jnp.where(col_id == 0, 0.0, up)
                down = jnp.where(col_id == nz - 1, 0.0, down)
            coef[plane, 1 + 2 * dim] = up
            coef[plane, 2 + 2 * dim] = down
        coef[plane, 0] = centre
        return carry

    lax.fori_loop(0, 6, make_coef, 0)

    def one_probe(i, carry):
        def tangent(plane, inner):
            u = fwd_state[i, plane + 1]
            out = coef[plane, 0] * u
            out += coef[plane, 1] * fwd_state[i, plane]
            out += coef[plane, 2] * fwd_state[i, plane + 2]
            out += coef[plane, 3] * pltpu.roll(u, 1, 0)
            out += coef[plane, 4] * pltpu.roll(u, ny - 1, 0)
            out += coef[plane, 5] * pltpu.roll(u, 1, 1)
            out += coef[plane, 6] * pltpu.roll(u, nz - 1, 1)
            weighted[plane] = field[plane, 3] * out
            return inner

        lax.fori_loop(0, 6, tangent, 0)

        def adjoint(at, inner):
            plane = at + 1
            v = weighted[plane]
            out = coef[plane, 0] * v + field[plane, 4] * fwd_state[i, plane + 1]
            out += coef[plane + 1, 1] * weighted[plane + 1]
            out += coef[plane - 1, 2] * weighted[plane - 1]
            out += pltpu.roll(coef[plane, 3] * v, ny - 1, 0)
            out += pltpu.roll(coef[plane, 4] * v, 1, 0)
            out += pltpu.roll(coef[plane, 5] * v, nz - 1, 1)
            out += pltpu.roll(coef[plane, 6] * v, 1, 1)
            image[i, at] = out
            return inner

        lax.fori_loop(0, 4, adjoint, 0)
        return carry

    def block_src(first, count, px, pp):
        return image.at[pl.ds(first, count), pl.ds(2 * px, 2), pl.ds(pp * band, band)]

    def block_dst(owner, first, count):
        return rows_ref.at[pl.ds(owner * half + first, count)]

    def rank_of(px, pp):
        return pp * 2 + px

    my_rank = rank_of(side, probe)

    def step_body(c, carry):
        @pl.when(c < chunks)
        def _():
            x_copy(c).wait_recv()

            @pl.when(relay_hi)
            def _():
                hi_copy(zf_src(c), c, zf_send).start()

            @pl.when(relay_lo)
            def _():
                lo_copy(zf_src(c), c, zf_send).start()

            @pl.when(c + window < chunks)
            def _():
                launch(c + window)

        @pl.when(c > 0)
        def _():
            d = c - 1
            own_copy(d).wait()

            @pl.when(has_lo)
            def _():
                hi_copy(zf_src(d), d, zf_send).wait_recv()

            @pl.when(has_hi)
            def _():
                lo_copy(zf_src(d), d, zf_send).wait_recv()

            lax.fori_loop(d * per, (d + 1) * per, one_probe, 0)
            for step in range(1, n_peer):
                _, px, pp = peer(step)
                remote(
                    block_src(d * per, per, px, pp), block_dst(my_rank, d * per, per),
                    a_send.at[step], a_recv.at[n_peer - step], (base + px, pp),
                ).start()
            pltpu.make_async_copy(
                block_src(d * per, per, side, probe), block_dst(my_rank, d * per, per), a_own
            ).start()

        return carry

    lax.fori_loop(0, chunks + 1, step_body, 0)

    for step in range(1, n_peer):
        _, px, pp = peer(step)
        remote(
            block_src(0, half, px, pp), block_dst(rank_of(px, pp), 0, half),
            a_send.at[step], a_recv.at[step], (base + px, pp),
        ).wait()
    pltpu.make_async_copy(
        block_src(0, half, side, probe), block_dst(my_rank, 0, half), a_own
    ).wait()

    y_copy = pltpu.make_async_copy(rows_ref, y_out, y_sem)
    y_copy.start()

    count = rows_ref.shape[0]
    depth = rows_ref.shape[1] * band
    flat = rows_ref.reshape(count * depth, nz)
    gram_part[...] = jnp.zeros_like(gram_part)

    def gram_step(t, carry):
        cols = jnp.concatenate(
            [flat[pl.ds(t * 8 + r, count, stride=depth), :] for r in range(8)], axis=1
        )
        gram_part[...] += lax.dot_general(
            cols, cols, (((1,), (1,)), ((), ())), precision=highest,
            preferred_element_type=jnp.float32,
        )
        return carry

    lax.fori_loop(0, depth // 8, gram_step, 0)

    share = count // n_peer

    def r_copy(step):
        other, px, pp = peer(step)
        return remote(
            gram_part.at[pl.ds(other * share, share)], reduce_buf.at[mine],
            r_send.at[step], r_recv.at[n_peer - step], (base + px, pp),
        )

    for step in range(1, n_peer):
        r_copy(step).start()
    reduce_buf[mine] = gram_part[pl.ds(pl.multiple_of(mine * share, share), share)]
    for step in range(1, n_peer):
        r_copy(step).wait_recv()
    group_buf[group] = jnp.sum(reduce_buf[...], axis=0)

    def g_copy(step):
        other, at = sister(step)
        return remote(
            group_buf.at[group], group_buf.at[group],
            g_send.at[step], g_recv.at[n_group - step], (at, probe),
        )

    for step in range(1, n_group):
        g_copy(step).start()
    for step in range(1, n_group):
        g_copy(step).wait_recv()
    total[pl.ds(pl.multiple_of(mine * share, share), share)] = jnp.sum(group_buf[...], axis=0)

    def t_copy(step):
        _, px, pp = peer(step)
        return remote(
            total.at[pl.ds(mine * share, share)], total.at[pl.ds(mine * share, share)],
            t_send.at[step], t_recv.at[n_peer - step], (base + px, pp),
        )

    for step in range(1, n_peer):
        t_copy(step).start()
    for step in range(1, n_peer):
        t_copy(step).wait_recv()
    gram_out[...] = total[...]

    for step in range(1, n_peer):
        r_copy(step).wait_send()
        t_copy(step).wait_send()
    for step in range(1, n_group):
        g_copy(step).wait_send()
    x_f.wait_send()

    @pl.when(direct_lo)
    def _():
        z_low(fields_ref.at[0, pl.ds(0, 4)], f_zds).wait_send()

    @pl.when(direct_hi)
    def _():
        z_high(fields_ref.at[1, pl.ds(0, 4)], f_zds).wait_send()

    @pl.when(relay_hi)
    def _():
        z_high(field.at[4, pl.ds(0, 4)], f_zfs).wait_send()

    @pl.when(relay_lo)
    def _():
        z_low(field.at[1, pl.ds(0, 4)], f_zfs).wait_send()

    def drain(c, carry):
        x_copy(c).wait_send()

        @pl.when(direct_lo)
        def _():
            lo_copy(zd_src(c), c, zd_send).wait_send()

        @pl.when(direct_hi)
        def _():
            hi_copy(zd_src(c), c, zd_send).wait_send()

        @pl.when(relay_hi)
        def _():
            hi_copy(zf_src(c), c, zf_send).wait_send()

        @pl.when(relay_lo)
        def _():
            lo_copy(zf_src(c), c, zf_send).wait_send()

        return carry

    lax.fori_loop(0, chunks, drain, 0)
    y_copy.wait()


def exchange(probes, fields, n_space, n_probe, chunks=8, window=2):
    local, planes, ny, nz = probes.shape
    count = local * n_probe
    half = local // 2
    band = ny // n_probe
    n_peer, n_group = 2 * n_probe, n_space // 2
    share = count // n_peer
    f32 = jnp.float32
    dma = pltpu.SemaphoreType.DMA
    return pl.pallas_call(
        functools.partial(exchange_kernel, n_space, n_probe, chunks, window),
        out_shape=(
            jax.ShapeDtypeStruct((count, planes, band, nz), f32),
            jax.ShapeDtypeStruct((count, count), f32),
        ),
        in_specs=[pl.BlockSpec(memory_space=pl.ANY)] * 2,
        out_specs=(
            pl.BlockSpec(memory_space=pl.ANY),
            pl.BlockSpec(memory_space=pltpu.VMEM),
        ),
        scratch_shapes=[
            pltpu.VMEM((6, 5, ny, nz), f32),
            pltpu.VMEM((half, 8, ny, nz), f32),
            pltpu.VMEM((6, 7, ny, nz), f32),
            pltpu.VMEM((6, ny, nz), f32),
            pltpu.VMEM((half, 4, ny, nz), f32),
            pltpu.VMEM((count, planes, band, nz), f32),
            pltpu.VMEM((count, count), f32),
            pltpu.VMEM((n_peer, share, count), f32),
            pltpu.VMEM((n_group, share, count), f32),
            pltpu.VMEM((count, count), f32),
        ]
        + [dma((chunks,))] * 7
        + [dma(())] * 7
        + [dma((n_peer,)), dma((n_peer,)), dma(())]
        + [dma((n_peer,)), dma((n_peer,)), dma((n_group,)), dma((n_group,))]
        + [dma((n_peer,)), dma((n_peer,)), dma(())],
        compiler_params=pltpu.CompilerParams(
            collective_id=0, has_side_effects=True, vmem_limit_bytes=48 * 1024 * 1024
        ),
        name="exchange",
    )(probes, fields)


def basis_kernel(inverse_ref, y_ref, out_ref):
    count, rows, nz = y_ref.shape
    flat = y_ref.reshape(count * rows, nz)
    result_flat = out_ref.reshape(count * rows, nz)
    cols = jnp.concatenate(
        [flat[pl.ds(r, count, stride=rows), :] for r in range(rows)], axis=1
    )
    result = jnp.dot(
        inverse_ref[...], cols, precision=highest, preferred_element_type=jnp.float32
    )
    for r in range(rows):
        result_flat[pl.ds(r, count, stride=rows), :] = result[:, r * nz : (r + 1) * nz]


def basis(inverse, y_rows, rows=8):
    count, depth, nz = y_rows.shape
    block = pl.BlockSpec((count, rows, nz), lambda i: (0, i, 0))
    return pl.pallas_call(
        basis_kernel,
        grid=(depth // rows,),
        out_shape=jax.ShapeDtypeStruct(y_rows.shape, jnp.float32),
        in_specs=[pl.BlockSpec((count, count), lambda i: (0, 0)), block],
        out_specs=block,
        compiler_params=pltpu.CompilerParams(vmem_limit_bytes=32 * 1024 * 1024),
        name="basis",
    )(inverse, y_rows)


def per_device(probes, winds, wind_step, obs_weight, prior_weight):
    n_space, n_probe = lax.axis_size("space"), lax.axis_size("probe")
    wind_now = select_wind(winds, wind_step)
    fields = jnp.concatenate([wind_now, obs_weight[None], prior_weight[None]], axis=0)
    fields = jnp.swapaxes(fields, 0, 1)
    image, gram_matrix = exchange(probes, fields, n_space, n_probe)
    low_factor = jnp.linalg.cholesky(gram_matrix)
    cells_all = image[0].size * n_space * n_probe
    norm_scale = math.sqrt(cells_all)
    eye = jnp.eye(low_factor.shape[0], dtype=jnp.float32)
    inverse = jax.scipy.linalg.solve_triangular(low_factor, eye, lower=True) * norm_scale
    count, planes, band, nz = image.shape
    basis_out = basis(inverse, image.reshape(count, planes * band, nz)).reshape(image.shape)
    return (basis_out, low_factor.T / norm_scale)


def solution(mesh):
    placed = (
        P("probe", "space", None, None),
        P(None, None, "space", None, None),
        P("space"),
        P("space", None, None),
        P("space", None, None),
    )
    return jax.shard_map(
        per_device,
        mesh=mesh,
        in_specs=placed,
        out_specs=(P(None, "space", "probe", None), P()),
        check_vma=False,
    )
```

```python
import functools
import math

import jax
import jax.numpy as jnp
from jax import lax
from jax.experimental import pallas as pl
from jax.experimental.pallas import tpu as pltpu
from jax.sharding import PartitionSpec as P

diffusion = 0.1
MESH = pl.DeviceIdType.MESH
highest = lax.Precision.HIGHEST


def select_wind(winds, wind_step):
    levels = jnp.arange(winds.shape[0], dtype=jnp.int32)
    picked = levels[:, None] == wind_step[None, :]
    return jnp.sum(jnp.where(picked[:, None, :, None, None], winds, jnp.zeros_like(winds)), axis=0)


def exchange_kernel(
    n_space, n_probe, chunks, window,
    probes_ref, fields_ref, y_out, gram_out,
    field, fwd_state, coef, weighted, image, rows_ref, gram_acc, gram_part, reduce_buf, group_buf, total,
    own_sem, x_send, x_recv, zd_send, zf_send, lo_recv, hi_recv,
    f_own, f_xs, f_xr, f_zds, f_zfs, f_lor, f_hir,
    a_send, a_recv, a_own, r_send, r_recv, g_send, g_recv, t_send, t_recv, y_sem,
):
    space = lax.axis_index("space")
    probe = lax.axis_index("probe")
    side = lax.rem(space, 2)
    partner = space + 1 - 2 * side
    group = lax.div(space, 2)
    n_group = n_space // 2
    base = space - side
    n_peer = 2 * n_probe
    mine = side * n_probe + probe
    half = probes_ref.shape[0] // 2
    per = half // chunks
    ny, nz = probes_ref.shape[2], probes_ref.shape[3]
    band = ny // n_probe
    below, above = space - 2, space + 2
    has_lo, has_hi = group > 0, group < n_group - 1

    def peer(step):
        other = lax.rem(mine + step, n_peer)
        return other, lax.div(other, n_probe), lax.rem(other, n_probe)

    def sister(step):
        other = lax.rem(group + step, n_group)
        return other, 2 * other + side

    barrier = pltpu.get_barrier_semaphore()
    for step in range(1, n_peer):
        _, px, pp = peer(step)
        pl.semaphore_signal(barrier, inc=1, device_id=(base + px, pp), device_id_type=MESH)
    for step in range(1, n_group):
        pl.semaphore_signal(
            barrier, inc=1, device_id=(sister(step)[1], probe), device_id_type=MESH
        )
    pl.semaphore_wait(barrier, n_peer + n_group - 2)

    def remote(src, dst, send, recv, dev):
        return pltpu.make_async_remote_copy(
            src_ref=src, dst_ref=dst, send_sem=send, recv_sem=recv,
            device_id=dev, device_id_type=MESH,
        )

    own_plane = 2 + 2 * side
    got_plane = 4 - 2 * side

    own_f = pltpu.make_async_copy(fields_ref, field.at[pl.ds(1 + 2 * side, 2)], f_own)
    own_f.start()
    x_f = remote(fields_ref, field.at[pl.ds(1 + 2 * side, 2)], f_xs, f_xr, (partner, probe))
    x_f.start()

    def z_low(src, send):
        return remote(src, field.at[5, pl.ds(0, 4)], send, f_hir, (below, probe))

    def z_high(src, send):
        return remote(src, field.at[0, pl.ds(0, 4)], send, f_lor, (above, probe))

    direct_lo = (side == 0) & has_lo
    direct_hi = (side == 1) & has_hi
    relay_hi = (side == 0) & has_hi
    relay_lo = (side == 1) & has_lo

    @pl.when(direct_lo)
    def _():
        z_low(fields_ref.at[0, pl.ds(0, 4)], f_zds).start()

    @pl.when(direct_hi)
    def _():
        z_high(fields_ref.at[1, pl.ds(0, 4)], f_zds).start()

    def chunk_at(c):
        return pl.ds(c * per, per)

    def x_copy(c):
        return remote(
            probes_ref.at[pl.ds((1 - side) * half + c * per, per)],
            fwd_state.at[chunk_at(c), pl.ds(own_plane, 2)],
            x_send.at[c], x_recv.at[c], (partner, probe),
        )

    def own_copy(c):
        return pltpu.make_async_copy(
            probes_ref.at[pl.ds(side * half + c * per, per)],
            fwd_state.at[chunk_at(c), pl.ds(own_plane, 2)],
            own_sem.at[c],
        )

    def zd_src(c):
        return probes_ref.at[pl.ds(side * half + c * per, per)]

    def zf_src(c):
        return fwd_state.at[chunk_at(c), pl.ds(got_plane, 2)]

    def lo_copy(src, c, send):
        return remote(
            src, fwd_state.at[chunk_at(c), pl.ds(6, 2)], send.at[c], hi_recv.at[c], (below, probe)
        )

    def hi_copy(src, c, send):
        return remote(
            src, fwd_state.at[chunk_at(c), pl.ds(0, 2)], send.at[c], lo_recv.at[c], (above, probe)
        )

    def launch(c):
        x_copy(c).start()
        own_copy(c).start()

        @pl.when(direct_lo)
        def _():
            lo_copy(zd_src(c), c, zd_send).start()

        @pl.when(direct_hi)
        def _():
            hi_copy(zd_src(c), c, zd_send).start()

    for c in range(window):
        launch(c)

    @pl.when(jnp.logical_not(has_lo))
    def _():
        field[0] = jnp.zeros(field.shape[1:], jnp.float32)

        def clear(i, carry):
            fwd_state[i, pl.ds(0, 2)] = jnp.zeros((2, ny, nz), jnp.float32)
            return carry

        lax.fori_loop(0, half, clear, 0)

    @pl.when(jnp.logical_not(has_hi))
    def _():
        field[5] = jnp.zeros(field.shape[1:], jnp.float32)

        def clear(i, carry):
            fwd_state[i, pl.ds(6, 2)] = jnp.zeros((2, ny, nz), jnp.float32)
            return carry

        lax.fori_loop(0, half, clear, 0)

    x_f.wait_recv()

    @pl.when(relay_hi)
    def _():
        z_high(field.at[4, pl.ds(0, 4)], f_zfs).start()

    @pl.when(relay_lo)
    def _():
        z_low(field.at[1, pl.ds(0, 4)], f_zfs).start()

    own_f.wait()

    @pl.when(has_lo)
    def _():
        z_high(field.at[0, pl.ds(0, 4)], f_zfs).wait_recv()

    @pl.when(has_hi)
    def _():
        z_low(field.at[5, pl.ds(0, 4)], f_zfs).wait_recv()

    row_id = lax.broadcasted_iota(jnp.int32, (ny, nz), 0)
    col_id = lax.broadcasted_iota(jnp.int32, (ny, nz), 1)

    def make_coef(plane, carry):
        centre = jnp.full((ny, nz), 1.0 - 6.0 * diffusion, jnp.float32)
        for dim in range(3):
            speed = field[plane, dim]
            pos, neg = jnp.maximum(speed, 0.0), jnp.minimum(speed, 0.0)
            centre = centre - pos + neg
            up, down = pos + diffusion, diffusion - neg
            if dim == 1:
                up = jnp.where(row_id == 0, 0.0, up)
                down = jnp.where(row_id == ny - 1, 0.0, down)
            if dim == 2:
                up = jnp.where(col_id == 0, 0.0, up)
                down = jnp.where(col_id == nz - 1, 0.0, down)
            coef[plane, 1 + 2 * dim] = up
            coef[plane, 2 + 2 * dim] = down
        coef[plane, 0] = centre
        return carry

    lax.fori_loop(0, 6, make_coef, 0)

    def one_probe(i, carry):
        def tangent(plane, inner):
            u = fwd_state[i, plane + 1]
            out = coef[plane, 0] * u
            out += coef[plane, 1] * fwd_state[i, plane]
            out += coef[plane, 2] * fwd_state[i, plane + 2]
            out += coef[plane, 3] * pltpu.roll(u, 1, 0)
            out += coef[plane, 4] * pltpu.roll(u, ny - 1, 0)
            out += coef[plane, 5] * pltpu.roll(u, 1, 1)
            out += coef[plane, 6] * pltpu.roll(u, nz - 1, 1)
            weighted[plane] = field[plane, 3] * out
            return inner

        lax.fori_loop(0, 6, tangent, 0)

        def adjoint(at, inner):
            plane = at + 1
            v = weighted[plane]
            out = coef[plane, 0] * v + field[plane, 4] * fwd_state[i, plane + 1]
            out += coef[plane + 1, 1] * weighted[plane + 1]
            out += coef[plane - 1, 2] * weighted[plane - 1]
            out += pltpu.roll(coef[plane, 3] * v, ny - 1, 0)
            out += pltpu.roll(coef[plane, 4] * v, 1, 0)
            out += pltpu.roll(coef[plane, 5] * v, nz - 1, 1)
            out += pltpu.roll(coef[plane, 6] * v, 1, 1)
            image[i, at] = out
            return inner

        lax.fori_loop(0, 4, adjoint, 0)
        return carry

    def block_src(first, count, px, pp):
        return image.at[pl.ds(first, count), pl.ds(2 * px, 2), pl.ds(pp * band, band)]

    def block_dst(owner, first, count):
        return rows_ref.at[pl.ds(owner * half + first, count)]

    def rank_of(px, pp):
        return pp * 2 + px

    my_rank = rank_of(side, probe)

    def step_body(c, carry):
        @pl.when(c < chunks)
        def _():
            x_copy(c).wait_recv()

            @pl.when(relay_hi)
            def _():
                hi_copy(zf_src(c), c, zf_send).start()

            @pl.when(relay_lo)
            def _():
                lo_copy(zf_src(c), c, zf_send).start()

            @pl.when(c + window < chunks)
            def _():
                launch(c + window)

        @pl.when(c > 0)
        def _():
            d = c - 1
            own_copy(d).wait()

            @pl.when(has_lo)
            def _():
                hi_copy(zf_src(d), d, zf_send).wait_recv()

            @pl.when(has_hi)
            def _():
                lo_copy(zf_src(d), d, zf_send).wait_recv()

            lax.fori_loop(d * per, (d + 1) * per, one_probe, 0)
            for step in range(1, n_peer):
                _, px, pp = peer(step)
                remote(
                    block_src(d * per, per, px, pp), block_dst(my_rank, d * per, per),
                    a_send.at[step], a_recv.at[n_peer - step], (base + px, pp),
                ).start()
            pltpu.make_async_copy(
                block_src(d * per, per, side, probe), block_dst(my_rank, d * per, per), a_own
            ).start()

        return carry

    lax.fori_loop(0, chunks + 1, step_body, 0)

    for step in range(1, n_peer):
        _, px, pp = peer(step)
        remote(
            block_src(0, half, px, pp), block_dst(rank_of(px, pp), 0, half),
            a_send.at[step], a_recv.at[step], (base + px, pp),
        ).wait()
    pltpu.make_async_copy(
        block_src(0, half, side, probe), block_dst(my_rank, 0, half), a_own
    ).wait()

    y_copy = pltpu.make_async_copy(rows_ref, y_out, y_sem)
    y_copy.start()

    count = rows_ref.shape[0]
    depth = rows_ref.shape[1] * band
    flat = rows_ref.reshape(count * depth, nz)
    gram_acc[...] = jnp.zeros_like(gram_acc)

    def gram_step(t, carry):
        cols = jnp.concatenate(
            [flat[pl.ds(t * 8 + r, count, stride=depth), :] for r in range(8)], axis=1
        )
        both = jnp.concatenate(split(cols), axis=0)
        gram_acc[...] += lax.dot_general(
            both, both, (((1,), (1,)), ((), ())), preferred_element_type=jnp.float32
        )
        return carry

    lax.fori_loop(0, depth // 8, gram_step, 0)
    across = gram_acc[:count, count:] + gram_acc[count:, :count]
    gram_part[...] = gram_acc[:count, :count] + (across + gram_acc[count:, count:])

    share = count // n_peer

    def r_copy(step):
        other, px, pp = peer(step)
        return remote(
            gram_part.at[pl.ds(other * share, share)], reduce_buf.at[mine],
            r_send.at[step], r_recv.at[n_peer - step], (base + px, pp),
        )

    for step in range(1, n_peer):
        r_copy(step).start()
    reduce_buf[mine] = gram_part[pl.ds(pl.multiple_of(mine * share, share), share)]
    for step in range(1, n_peer):
        r_copy(step).wait_recv()
    group_buf[group] = jnp.sum(reduce_buf[...], axis=0)

    def g_copy(step):
        other, at = sister(step)
        return remote(
            group_buf.at[group], group_buf.at[group],
            g_send.at[step], g_recv.at[n_group - step], (at, probe),
        )

    for step in range(1, n_group):
        g_copy(step).start()
    for step in range(1, n_group):
        g_copy(step).wait_recv()
    total[pl.ds(pl.multiple_of(mine * share, share), share)] = jnp.sum(group_buf[...], axis=0)

    def t_copy(step):
        _, px, pp = peer(step)
        return remote(
            total.at[pl.ds(mine * share, share)], total.at[pl.ds(mine * share, share)],
            t_send.at[step], t_recv.at[n_peer - step], (base + px, pp),
        )

    for step in range(1, n_peer):
        t_copy(step).start()
    for step in range(1, n_peer):
        t_copy(step).wait_recv()
    gram_out[...] = total[...]

    for step in range(1, n_peer):
        r_copy(step).wait_send()
        t_copy(step).wait_send()
    for step in range(1, n_group):
        g_copy(step).wait_send()
    x_f.wait_send()

    @pl.when(direct_lo)
    def _():
        z_low(fields_ref.at[0, pl.ds(0, 4)], f_zds).wait_send()

    @pl.when(direct_hi)
    def _():
        z_high(fields_ref.at[1, pl.ds(0, 4)], f_zds).wait_send()

    @pl.when(relay_hi)
    def _():
        z_high(field.at[4, pl.ds(0, 4)], f_zfs).wait_send()

    @pl.when(relay_lo)
    def _():
        z_low(field.at[1, pl.ds(0, 4)], f_zfs).wait_send()

    def drain(c, carry):
        x_copy(c).wait_send()

        @pl.when(direct_lo)
        def _():
            lo_copy(zd_src(c), c, zd_send).wait_send()

        @pl.when(direct_hi)
        def _():
            hi_copy(zd_src(c), c, zd_send).wait_send()

        @pl.when(relay_hi)
        def _():
            hi_copy(zf_src(c), c, zf_send).wait_send()

        @pl.when(relay_lo)
        def _():
            lo_copy(zf_src(c), c, zf_send).wait_send()

        return carry

    lax.fori_loop(0, chunks, drain, 0)
    y_copy.wait()


def exchange(probes, fields, n_space, n_probe, chunks=8, window=2):
    local, planes, ny, nz = probes.shape
    count = local * n_probe
    half = local // 2
    band = ny // n_probe
    n_peer, n_group = 2 * n_probe, n_space // 2
    share = count // n_peer
    f32 = jnp.float32
    dma = pltpu.SemaphoreType.DMA
    return pl.pallas_call(
        functools.partial(exchange_kernel, n_space, n_probe, chunks, window),
        out_shape=(
            jax.ShapeDtypeStruct((count, planes, band, nz), f32),
            jax.ShapeDtypeStruct((count, count), f32),
        ),
        in_specs=[pl.BlockSpec(memory_space=pl.ANY)] * 2,
        out_specs=(
            pl.BlockSpec(memory_space=pl.ANY),
            pl.BlockSpec(memory_space=pltpu.VMEM),
        ),
        scratch_shapes=[
            pltpu.VMEM((6, 5, ny, nz), f32),
            pltpu.VMEM((half, 8, ny, nz), f32),
            pltpu.VMEM((6, 7, ny, nz), f32),
            pltpu.VMEM((6, ny, nz), f32),
            pltpu.VMEM((half, 4, ny, nz), f32),
            pltpu.VMEM((count, planes, band, nz), f32),
            pltpu.VMEM((2 * count, 2 * count), f32),
            pltpu.VMEM((count, count), f32),
            pltpu.VMEM((n_peer, share, count), f32),
            pltpu.VMEM((n_group, share, count), f32),
            pltpu.VMEM((count, count), f32),
        ]
        + [dma((chunks,))] * 7
        + [dma(())] * 7
        + [dma((n_peer,)), dma((n_peer,)), dma(())]
        + [dma((n_peer,)), dma((n_peer,)), dma((n_group,)), dma((n_group,))]
        + [dma((n_peer,)), dma((n_peer,)), dma(())],
        compiler_params=pltpu.CompilerParams(
            collective_id=0, has_side_effects=True, vmem_limit_bytes=48 * 1024 * 1024
        ),
        name="exchange",
    )(probes, fields)


def split(values):
    high = values.astype(jnp.bfloat16)
    low = (values - high.astype(jnp.float32)).astype(jnp.bfloat16)
    return high, low


def factor(gram_ref, work, n, rows=8):
    work[:, :n] = gram_ref[...]
    row_id = lax.broadcasted_iota(jnp.int32, (n, n), 0)
    col_id = lax.broadcasted_iota(jnp.int32, (n, n), 1)
    work[:, n:] = jnp.where(row_id == col_id, 1.0, 0.0)
    sub = lax.broadcasted_iota(jnp.int32, (rows, n), 0)
    lane = lax.broadcasted_iota(jnp.int32, (rows, n), 1)

    def panel_step(at, carry):
        start = pl.multiple_of(at * rows, rows)
        left = pltpu.roll(work[pl.ds(start, rows), :n], lax.rem(n - start, n), 1)
        right = work[pl.ds(start, rows), n:]
        for j in range(rows):
            col = jnp.broadcast_to(left[:, j : j + 1], (rows, n))
            pivot = jnp.broadcast_to(col[j : j + 1, :], (rows, n))
            scale = lax.rsqrt(pivot)
            scale = scale * (1.5 - 0.5 * (pivot * scale) * scale)
            row_left = jnp.broadcast_to(left[j : j + 1, :], (rows, n)) * scale
            row_right = jnp.broadcast_to(right[j : j + 1, :], (rows, n)) * scale
            times = jnp.where(sub > j, col * scale, 0.0)
            left = jnp.where(sub == j, row_left, left - times * row_left)
            right = jnp.where(sub == j, row_right, right - times * row_right)
        left = pltpu.roll(left, start, 1)
        ahead = jnp.where(lane >= start + rows, left, 0.0)
        both = jnp.concatenate([left, right], axis=1)
        work[...] -= lax.dot_general(
            ahead, both, (((0,), (0,)), ((), ())), precision=highest,
            preferred_element_type=jnp.float32,
        )
        work[pl.ds(start, rows), :] = both
        return carry

    lax.fori_loop(0, n // rows, panel_step, 0)
    upper = jnp.where(row_id <= col_id, work[:, :n], 0.0)
    return upper, work[:, n:]


def basis_kernel(
    norm_scale, gram_ref, y_hbm, out_hbm, factor_ref, work, y_ref, out_ref, in_sem, out_sem
):
    count, depth, nz = y_ref.shape
    fetch = pltpu.make_async_copy(y_hbm, y_ref, in_sem)
    fetch.start()
    upper, inverse = factor(gram_ref, work, count)
    factor_ref[...] = upper / norm_scale
    high, low = split(inverse * norm_scale)
    left = jnp.concatenate([high, low, high, low], axis=1)
    flat = y_ref.reshape(count * depth, nz)
    result_flat = out_ref.reshape(count * depth, nz)
    rows = 8
    fetch.wait()

    def store(t):
        part = pl.ds(pl.multiple_of(t * rows, rows), rows)
        return pltpu.make_async_copy(out_ref.at[:, part], out_hbm.at[:, part], out_sem.at[t])

    def block_step(t, carry):
        cols = jnp.concatenate(
            [flat[pl.ds(t * rows + r, count, stride=depth), :] for r in range(rows)], axis=1
        )
        y_high, y_low = split(cols)
        right = jnp.concatenate([y_high, y_high, y_low, y_low], axis=0)
        result = jnp.dot(left, right, preferred_element_type=jnp.float32)
        for r in range(rows):
            result_flat[pl.ds(t * rows + r, count, stride=depth), :] = result[
                :, r * nz : (r + 1) * nz
            ]
        store(t).start()
        return carry

    lax.fori_loop(0, depth // rows, block_step, 0)

    def drain(t, carry):
        store(t).wait()
        return carry

    lax.fori_loop(0, depth // rows, drain, 0)


def basis(gram_matrix, y_rows, norm_scale):
    count, depth, nz = y_rows.shape
    f32 = jnp.float32
    vmem = pl.BlockSpec(memory_space=pltpu.VMEM)
    hbm = pl.BlockSpec(memory_space=pl.ANY)
    return pl.pallas_call(
        functools.partial(basis_kernel, norm_scale),
        out_shape=(
            jax.ShapeDtypeStruct(y_rows.shape, f32),
            jax.ShapeDtypeStruct(gram_matrix.shape, f32),
        ),
        in_specs=[vmem, hbm],
        out_specs=(hbm, vmem),
        scratch_shapes=[
            pltpu.VMEM((count, 2 * count), f32),
            pltpu.VMEM(y_rows.shape, f32),
            pltpu.VMEM(y_rows.shape, f32),
            pltpu.SemaphoreType.DMA(()),
            pltpu.SemaphoreType.DMA((depth // 8,)),
        ],
        compiler_params=pltpu.CompilerParams(vmem_limit_bytes=56 * 1024 * 1024),
        name="basis",
    )(gram_matrix, y_rows)


def per_device(probes, winds, wind_step, obs_weight, prior_weight):
    n_space, n_probe = lax.axis_size("space"), lax.axis_size("probe")
    wind_now = select_wind(winds, wind_step)
    fields = jnp.concatenate([wind_now, obs_weight[None], prior_weight[None]], axis=0)
    fields = jnp.swapaxes(fields, 0, 1)
    image, gram_matrix = exchange(probes, fields, n_space, n_probe)
    count, planes, band, nz = image.shape
    norm_scale = math.sqrt(planes * band * nz * n_space * n_probe)
    basis_out, r_factor = basis(
        gram_matrix, image.reshape(count, planes * band, nz), norm_scale
    )
    return (basis_out.reshape(image.shape), r_factor)


def solution(mesh):
    placed = (
        P("probe", "space", None, None),
        P(None, None, "space", None, None),
        P("space"),
        P("space", None, None),
        P("space", None, None),
    )
    return jax.shard_map(
        per_device,
        mesh=mesh,
        in_specs=placed,
        out_specs=(P(None, "space", "probe", None), P()),
        check_vma=False,
    )
```

```python
import functools
import math

import jax
import jax.numpy as jnp
from jax import lax
from jax.experimental import pallas as pl
from jax.experimental.pallas import tpu as pltpu
from jax.sharding import PartitionSpec as P

diffusion = 0.1
MESH = pl.DeviceIdType.MESH
highest = lax.Precision.HIGHEST


def select_wind(winds, wind_step):
    levels = jnp.arange(winds.shape[0], dtype=jnp.int32)
    picked = levels[:, None] == wind_step[None, :]
    return jnp.sum(jnp.where(picked[:, None, :, None, None], winds, jnp.zeros_like(winds)), axis=0)


def exchange_kernel(
    n_space, n_probe, chunks, window,
    probes_ref, fields_ref, y_out, gram_out,
    field, fwd_state, coef, weighted, image, rows_ref, gram_acc, gram_part, reduce_buf, group_buf, total,
    own_sem, x_send, x_recv, zd_send, zf_send, lo_recv, hi_recv,
    f_own, f_xs, f_xr, f_zds, f_zfs, f_lor, f_hir, s_send, s_recv,
    a_send, a_recv, a_own, r_send, r_recv, g_send, g_recv, t_send, t_recv, y_sem,
):
    space = lax.axis_index("space")
    probe = lax.axis_index("probe")
    side = lax.rem(space, 2)
    partner = space + 1 - 2 * side
    group = lax.div(space, 2)
    n_group = n_space // 2
    base = space - side
    n_peer = 2 * n_probe
    mine = side * n_probe + probe
    half = probes_ref.shape[0] // 2
    per = half // chunks
    ny, nz = probes_ref.shape[2], probes_ref.shape[3]
    band = ny // n_probe
    below, above = space - 2, space + 2
    has_lo, has_hi = group > 0, group < n_group - 1

    def peer(step):
        other = lax.rem(mine + step, n_peer)
        return other, lax.div(other, n_probe), lax.rem(other, n_probe)

    def sister(step):
        other = lax.rem(group + step, n_group)
        return other, 2 * other + side

    barrier = pltpu.get_barrier_semaphore()
    for step in range(1, n_peer):
        _, px, pp = peer(step)
        pl.semaphore_signal(barrier, inc=1, device_id=(base + px, pp), device_id_type=MESH)
    for step in range(1, n_group):
        pl.semaphore_signal(
            barrier, inc=1, device_id=(sister(step)[1], probe), device_id_type=MESH
        )
    pl.semaphore_wait(barrier, n_peer + n_group - 2)

    def remote(src, dst, send, recv, dev):
        return pltpu.make_async_remote_copy(
            src_ref=src, dst_ref=dst, send_sem=send, recv_sem=recv,
            device_id=dev, device_id_type=MESH,
        )

    own_plane = 2 + 2 * side
    got_plane = 4 - 2 * side

    band_at = pl.ds(probe * band, band)
    own_f = pltpu.make_async_copy(fields_ref, field.at[pl.ds(1 + 2 * side, 2)], f_own)
    own_f.start()
    x_f = remote(
        fields_ref.at[:, :, band_at], field.at[pl.ds(1 + 2 * side, 2), :, band_at],
        f_xs, f_xr, (partner, probe),
    )
    x_f.start()

    def z_low(src, plane, send):
        return remote(
            src.at[plane, pl.ds(0, 4), band_at], field.at[5, pl.ds(0, 4), band_at],
            send, f_hir, (below, probe),
        )

    def z_high(src, plane, send):
        return remote(
            src.at[plane, pl.ds(0, 4), band_at], field.at[0, pl.ds(0, 4), band_at],
            send, f_lor, (above, probe),
        )

    def share_copy(kind, step):
        if kind == 0:
            ref = field.at[pl.ds(3 - 2 * side, 2), :, band_at]
        else:
            ref = field.at[0 if kind == 1 else 5, pl.ds(0, 4), band_at]
        to = lax.rem(probe + step, n_probe)
        return remote(
            ref, ref, s_send.at[kind, step], s_recv.at[kind, n_probe - step], (space, to)
        )

    def share_start(kind):
        for step in range(1, n_probe):
            share_copy(kind, step).start()

    def share_wait(kind):
        for step in range(1, n_probe):
            share_copy(kind, step).wait_recv()

    def share_drain(kind):
        for step in range(1, n_probe):
            share_copy(kind, step).wait_send()

    direct_lo = (side == 0) & has_lo
    direct_hi = (side == 1) & has_hi
    relay_hi = (side == 0) & has_hi
    relay_lo = (side == 1) & has_lo

    @pl.when(direct_lo)
    def _():
        z_low(fields_ref, 0, f_zds).start()

    @pl.when(direct_hi)
    def _():
        z_high(fields_ref, 1, f_zds).start()

    def chunk_at(c):
        return pl.ds(c * per, per)

    def x_copy(c):
        return remote(
            probes_ref.at[pl.ds((1 - side) * half + c * per, per)],
            fwd_state.at[chunk_at(c), pl.ds(own_plane, 2)],
            x_send.at[c], x_recv.at[c], (partner, probe),
        )

    def own_copy(c):
        return pltpu.make_async_copy(
            probes_ref.at[pl.ds(side * half + c * per, per)],
            fwd_state.at[chunk_at(c), pl.ds(own_plane, 2)],
            own_sem.at[c],
        )

    def zd_src(c):
        return probes_ref.at[pl.ds(side * half + c * per, per)]

    def zf_src(c):
        return fwd_state.at[chunk_at(c), pl.ds(got_plane, 2)]

    def lo_copy(src, c, send):
        return remote(
            src, fwd_state.at[chunk_at(c), pl.ds(6, 2)], send.at[c], hi_recv.at[c], (below, probe)
        )

    def hi_copy(src, c, send):
        return remote(
            src, fwd_state.at[chunk_at(c), pl.ds(0, 2)], send.at[c], lo_recv.at[c], (above, probe)
        )

    def launch(c):
        x_copy(c).start()
        own_copy(c).start()

        @pl.when(direct_lo)
        def _():
            lo_copy(zd_src(c), c, zd_send).start()

        @pl.when(direct_hi)
        def _():
            hi_copy(zd_src(c), c, zd_send).start()

    for c in range(window):
        launch(c)

    @pl.when(jnp.logical_not(has_lo))
    def _():
        field[0] = jnp.zeros(field.shape[1:], jnp.float32)

        def clear(i, carry):
            fwd_state[i, pl.ds(0, 2)] = jnp.zeros((2, ny, nz), jnp.float32)
            return carry

        lax.fori_loop(0, half, clear, 0)

    @pl.when(jnp.logical_not(has_hi))
    def _():
        field[5] = jnp.zeros(field.shape[1:], jnp.float32)

        def clear(i, carry):
            fwd_state[i, pl.ds(6, 2)] = jnp.zeros((2, ny, nz), jnp.float32)
            return carry

        lax.fori_loop(0, half, clear, 0)

    x_f.wait_recv()

    @pl.when(relay_hi)
    def _():
        z_high(field, 4, f_zfs).start()

    @pl.when(relay_lo)
    def _():
        z_low(field, 1, f_zfs).start()

    share_start(0)

    @pl.when(has_lo)
    def _():
        z_high(field, 0, f_zfs).wait_recv()
        share_start(1)

    @pl.when(has_hi)
    def _():
        z_low(field, 5, f_zfs).wait_recv()
        share_start(2)

    own_f.wait()
    share_wait(0)

    @pl.when(has_lo)
    def _():
        share_wait(1)

    @pl.when(has_hi)
    def _():
        share_wait(2)

    row_id = lax.broadcasted_iota(jnp.int32, (ny, nz), 0)
    col_id = lax.broadcasted_iota(jnp.int32, (ny, nz), 1)

    def make_coef(plane, carry):
        centre = jnp.full((ny, nz), 1.0 - 6.0 * diffusion, jnp.float32)
        for dim in range(3):
            speed = field[plane, dim]
            pos, neg = jnp.maximum(speed, 0.0), jnp.minimum(speed, 0.0)
            centre = centre - pos + neg
            up, down = pos + diffusion, diffusion - neg
            if dim == 1:
                up = jnp.where(row_id == 0, 0.0, up)
                down = jnp.where(row_id == ny - 1, 0.0, down)
            if dim == 2:
                up = jnp.where(col_id == 0, 0.0, up)
                down = jnp.where(col_id == nz - 1, 0.0, down)
            coef[plane, 1 + 2 * dim] = up
            coef[plane, 2 + 2 * dim] = down
        coef[plane, 0] = centre
        return carry

    lax.fori_loop(0, 6, make_coef, 0)

    def one_probe(i, carry):
        def tangent(plane, inner):
            u = fwd_state[i, plane + 1]
            out = coef[plane, 0] * u
            out += coef[plane, 1] * fwd_state[i, plane]
            out += coef[plane, 2] * fwd_state[i, plane + 2]
            out += coef[plane, 3] * pltpu.roll(u, 1, 0)
            out += coef[plane, 4] * pltpu.roll(u, ny - 1, 0)
            out += coef[plane, 5] * pltpu.roll(u, 1, 1)
            out += coef[plane, 6] * pltpu.roll(u, nz - 1, 1)
            weighted[plane] = field[plane, 3] * out
            return inner

        lax.fori_loop(0, 6, tangent, 0)

        def adjoint(at, inner):
            plane = at + 1
            v = weighted[plane]
            out = coef[plane, 0] * v + field[plane, 4] * fwd_state[i, plane + 1]
            out += coef[plane + 1, 1] * weighted[plane + 1]
            out += coef[plane - 1, 2] * weighted[plane - 1]
            out += pltpu.roll(coef[plane, 3] * v, ny - 1, 0)
            out += pltpu.roll(coef[plane, 4] * v, 1, 0)
            out += pltpu.roll(coef[plane, 5] * v, nz - 1, 1)
            out += pltpu.roll(coef[plane, 6] * v, 1, 1)
            image[i, at] = out
            return inner

        lax.fori_loop(0, 4, adjoint, 0)
        return carry

    def block_src(first, count, px, pp):
        return image.at[pl.ds(first, count), pl.ds(2 * px, 2), pl.ds(pp * band, band)]

    def block_dst(owner, first, count):
        return rows_ref.at[pl.ds(owner * half + first, count)]

    def rank_of(px, pp):
        return pp * 2 + px

    my_rank = rank_of(side, probe)

    def step_body(c, carry):
        @pl.when(c < chunks)
        def _():
            x_copy(c).wait_recv()

            @pl.when(relay_hi)
            def _():
                hi_copy(zf_src(c), c, zf_send).start()

            @pl.when(relay_lo)
            def _():
                lo_copy(zf_src(c), c, zf_send).start()

            @pl.when(c + window < chunks)
            def _():
                launch(c + window)

        @pl.when(c > 0)
        def _():
            d = c - 1
            own_copy(d).wait()

            @pl.when(has_lo)
            def _():
                hi_copy(zf_src(d), d, zf_send).wait_recv()

            @pl.when(has_hi)
            def _():
                lo_copy(zf_src(d), d, zf_send).wait_recv()

            lax.fori_loop(d * per, (d + 1) * per, one_probe, 0)
            for step in range(1, n_peer):
                _, px, pp = peer(step)
                remote(
                    block_src(d * per, per, px, pp), block_dst(my_rank, d * per, per),
                    a_send.at[step], a_recv.at[n_peer - step], (base + px, pp),
                ).start()
            pltpu.make_async_copy(
                block_src(d * per, per, side, probe), block_dst(my_rank, d * per, per), a_own
            ).start()

        return carry

    lax.fori_loop(0, chunks + 1, step_body, 0)

    for step in range(1, n_peer):
        _, px, pp = peer(step)
        remote(
            block_src(0, half, px, pp), block_dst(rank_of(px, pp), 0, half),
            a_send.at[step], a_recv.at[step], (base + px, pp),
        ).wait()
    pltpu.make_async_copy(
        block_src(0, half, side, probe), block_dst(my_rank, 0, half), a_own
    ).wait()

    y_copy = pltpu.make_async_copy(rows_ref, y_out, y_sem)
    y_copy.start()

    count = rows_ref.shape[0]
    depth = rows_ref.shape[1] * band
    flat = rows_ref.reshape(count * depth, nz)
    gram_acc[...] = jnp.zeros_like(gram_acc)

    def gram_step(t, carry):
        cols = jnp.concatenate(
            [flat[pl.ds(t * 8 + r, count, stride=depth), :] for r in range(8)], axis=1
        )
        both = jnp.concatenate(split(cols), axis=0)
        gram_acc[...] += lax.dot_general(
            both, both, (((1,), (1,)), ((), ())), preferred_element_type=jnp.float32
        )
        return carry

    lax.fori_loop(0, depth // 8, gram_step, 0)
    across = gram_acc[:count, count:] + gram_acc[count:, :count]
    gram_part[...] = gram_acc[:count, :count] + (across + gram_acc[count:, count:])

    share = count // n_peer

    def r_copy(step):
        other, px, pp = peer(step)
        return remote(
            gram_part.at[pl.ds(other * share, share)], reduce_buf.at[mine],
            r_send.at[step], r_recv.at[n_peer - step], (base + px, pp),
        )

    for step in range(1, n_peer):
        r_copy(step).start()
    reduce_buf[mine] = gram_part[pl.ds(pl.multiple_of(mine * share, share), share)]
    for step in range(1, n_peer):
        r_copy(step).wait_recv()
    group_buf[group] = jnp.sum(reduce_buf[...], axis=0)

    def g_copy(step):
        other, at = sister(step)
        return remote(
            group_buf.at[group], group_buf.at[group],
            g_send.at[step], g_recv.at[n_group - step], (at, probe),
        )

    for step in range(1, n_group):
        g_copy(step).start()
    for step in range(1, n_group):
        g_copy(step).wait_recv()
    total[pl.ds(pl.multiple_of(mine * share, share), share)] = jnp.sum(group_buf[...], axis=0)

    def t_copy(step):
        _, px, pp = peer(step)
        return remote(
            total.at[pl.ds(mine * share, share)], total.at[pl.ds(mine * share, share)],
            t_send.at[step], t_recv.at[n_peer - step], (base + px, pp),
        )

    for step in range(1, n_peer):
        t_copy(step).start()
    for step in range(1, n_peer):
        t_copy(step).wait_recv()
    gram_out[...] = total[...]

    for step in range(1, n_peer):
        r_copy(step).wait_send()
        t_copy(step).wait_send()
    for step in range(1, n_group):
        g_copy(step).wait_send()
    x_f.wait_send()
    share_drain(0)

    @pl.when(has_lo)
    def _():
        share_drain(1)

    @pl.when(has_hi)
    def _():
        share_drain(2)

    @pl.when(direct_lo)
    def _():
        z_low(fields_ref, 0, f_zds).wait_send()

    @pl.when(direct_hi)
    def _():
        z_high(fields_ref, 1, f_zds).wait_send()

    @pl.when(relay_hi)
    def _():
        z_high(field, 4, f_zfs).wait_send()

    @pl.when(relay_lo)
    def _():
        z_low(field, 1, f_zfs).wait_send()

    def drain(c, carry):
        x_copy(c).wait_send()

        @pl.when(direct_lo)
        def _():
            lo_copy(zd_src(c), c, zd_send).wait_send()

        @pl.when(direct_hi)
        def _():
            hi_copy(zd_src(c), c, zd_send).wait_send()

        @pl.when(relay_hi)
        def _():
            hi_copy(zf_src(c), c, zf_send).wait_send()

        @pl.when(relay_lo)
        def _():
            lo_copy(zf_src(c), c, zf_send).wait_send()

        return carry

    lax.fori_loop(0, chunks, drain, 0)
    y_copy.wait()


def exchange(probes, fields, n_space, n_probe, chunks=8, window=2):
    local, planes, ny, nz = probes.shape
    count = local * n_probe
    half = local // 2
    band = ny // n_probe
    n_peer, n_group = 2 * n_probe, n_space // 2
    share = count // n_peer
    f32 = jnp.float32
    dma = pltpu.SemaphoreType.DMA
    return pl.pallas_call(
        functools.partial(exchange_kernel, n_space, n_probe, chunks, window),
        out_shape=(
            jax.ShapeDtypeStruct((count, planes, band, nz), f32),
            jax.ShapeDtypeStruct((count, count), f32),
        ),
        in_specs=[pl.BlockSpec(memory_space=pl.ANY)] * 2,
        out_specs=(
            pl.BlockSpec(memory_space=pl.ANY),
            pl.BlockSpec(memory_space=pltpu.VMEM),
        ),
        scratch_shapes=[
            pltpu.VMEM((6, 5, ny, nz), f32),
            pltpu.VMEM((half, 8, ny, nz), f32),
            pltpu.VMEM((6, 7, ny, nz), f32),
            pltpu.VMEM((6, ny, nz), f32),
            pltpu.VMEM((half, 4, ny, nz), f32),
            pltpu.VMEM((count, planes, band, nz), f32),
            pltpu.VMEM((2 * count, 2 * count), f32),
            pltpu.VMEM((count, count), f32),
            pltpu.VMEM((n_peer, share, count), f32),
            pltpu.VMEM((n_group, share, count), f32),
            pltpu.VMEM((count, count), f32),
        ]
        + [dma((chunks,))] * 7
        + [dma(())] * 7
        + [dma((3, n_probe))] * 2
        + [dma((n_peer,)), dma((n_peer,)), dma(())]
        + [dma((n_peer,)), dma((n_peer,)), dma((n_group,)), dma((n_group,))]
        + [dma((n_peer,)), dma((n_peer,)), dma(())],
        compiler_params=pltpu.CompilerParams(
            collective_id=0, has_side_effects=True, vmem_limit_bytes=48 * 1024 * 1024
        ),
        name="exchange",
    )(probes, fields)


def split(values):
    high = values.astype(jnp.bfloat16)
    low = (values - high.astype(jnp.float32)).astype(jnp.bfloat16)
    return high, low


def terms(values):
    found = []
    for _ in range(3):
        found.append(values.astype(jnp.bfloat16).astype(jnp.float32))
        values = values - found[-1]
    return found


def factor(gram_ref, work, n, rows=8):
    work[:, :n] = gram_ref[...]
    row_id = lax.broadcasted_iota(jnp.int32, (n, n), 0)
    col_id = lax.broadcasted_iota(jnp.int32, (n, n), 1)
    work[:, n:] = jnp.where(row_id == col_id, 1.0, 0.0)
    sub = lax.broadcasted_iota(jnp.int32, (rows, n), 0)
    lane = lax.broadcasted_iota(jnp.int32, (rows, n), 1)

    def panel_step(at, carry):
        start = pl.multiple_of(at * rows, rows)
        left = pltpu.roll(work[pl.ds(start, rows), :n], lax.rem(n - start, n), 1)
        right = work[pl.ds(start, rows), n:]
        columns = [jnp.broadcast_to(left[:, j : j + 1], (rows, n)) for j in range(rows)]
        pivots = columns[0]
        for j in range(rows):
            pivot = jnp.broadcast_to(columns[j][j : j + 1, :], (rows, n))
            times = jnp.where(sub > j, columns[j] * (1.0 / pivot), 0.0)
            pivots = jnp.where(sub == j, pivot, pivots)
            if j == rows - 1:
                break
            for i in range(j + 1, rows):
                columns[i] -= times * jnp.broadcast_to(columns[i][j : j + 1, :], (rows, n))
            left -= times * jnp.broadcast_to(left[j : j + 1, :], (rows, n))
            right -= times * jnp.broadcast_to(right[j : j + 1, :], (rows, n))
        scale = lax.rsqrt(pivots)
        scale = scale * (1.5 - 0.5 * (pivots * scale) * scale)
        left = pltpu.roll(left * scale, start, 1)
        right = right * scale
        ahead = jnp.where(lane >= start + rows, left, 0.0)
        both = jnp.concatenate([left, right], axis=1)
        a_terms, b_terms = terms(ahead), terms(both)
        pairs = ((0, 0), (0, 1), (1, 0), (1, 1), (0, 2), (2, 0))
        stacked_a = jnp.concatenate([a_terms[i] for i, _ in pairs], axis=0)
        stacked_b = jnp.concatenate([b_terms[i] for _, i in pairs], axis=0)
        work[...] -= lax.dot_general(
            stacked_a.astype(jnp.bfloat16), stacked_b.astype(jnp.bfloat16),
            (((0,), (0,)), ((), ())), preferred_element_type=jnp.float32,
        )
        work[pl.ds(start, rows), :] = both
        return carry

    lax.fori_loop(0, n // rows, panel_step, 0)
    upper = jnp.where(row_id <= col_id, work[:, :n], 0.0)
    return upper, work[:, n:]


def basis_kernel(
    norm_scale, gram_ref, y_hbm, out_hbm, factor_ref, work, y_ref, out_ref, in_sem, out_sem
):
    count, depth, nz = y_ref.shape
    fetch = pltpu.make_async_copy(y_hbm, y_ref, in_sem)
    fetch.start()
    upper, inverse = factor(gram_ref, work, count)
    factor_ref[...] = upper / norm_scale
    high, low = split(inverse * norm_scale)
    left = jnp.concatenate([high, low, high, low], axis=1)
    flat = y_ref.reshape(count * depth, nz)
    result_flat = out_ref.reshape(count * depth, nz)
    rows = 8
    fetch.wait()

    def store(t):
        part = pl.ds(pl.multiple_of(t * rows, rows), rows)
        return pltpu.make_async_copy(out_ref.at[:, part], out_hbm.at[:, part], out_sem.at[t])

    def block_step(t, carry):
        cols = jnp.concatenate(
            [flat[pl.ds(t * rows + r, count, stride=depth), :] for r in range(rows)], axis=1
        )
        y_high, y_low = split(cols)
        right = jnp.concatenate([y_high, y_high, y_low, y_low], axis=0)
        result = jnp.dot(left, right, preferred_element_type=jnp.float32)
        for r in range(rows):
            result_flat[pl.ds(t * rows + r, count, stride=depth), :] = result[
                :, r * nz : (r + 1) * nz
            ]
        store(t).start()
        return carry

    lax.fori_loop(0, depth // rows, block_step, 0)

    def drain(t, carry):
        store(t).wait()
        return carry

    lax.fori_loop(0, depth // rows, drain, 0)


def basis(gram_matrix, y_rows, norm_scale):
    count, depth, nz = y_rows.shape
    f32 = jnp.float32
    vmem = pl.BlockSpec(memory_space=pltpu.VMEM)
    hbm = pl.BlockSpec(memory_space=pl.ANY)
    return pl.pallas_call(
        functools.partial(basis_kernel, norm_scale),
        out_shape=(
            jax.ShapeDtypeStruct(y_rows.shape, f32),
            jax.ShapeDtypeStruct(gram_matrix.shape, f32),
        ),
        in_specs=[vmem, hbm],
        out_specs=(hbm, vmem),
        scratch_shapes=[
            pltpu.VMEM((count, 2 * count), f32),
            pltpu.VMEM(y_rows.shape, f32),
            pltpu.VMEM(y_rows.shape, f32),
            pltpu.SemaphoreType.DMA(()),
            pltpu.SemaphoreType.DMA((depth // 8,)),
        ],
        compiler_params=pltpu.CompilerParams(vmem_limit_bytes=56 * 1024 * 1024),
        name="basis",
    )(gram_matrix, y_rows)


def per_device(probes, winds, wind_step, obs_weight, prior_weight):
    n_space, n_probe = lax.axis_size("space"), lax.axis_size("probe")
    wind_now = select_wind(winds, wind_step)
    fields = jnp.concatenate([wind_now, obs_weight[None], prior_weight[None]], axis=0)
    fields = jnp.swapaxes(fields, 0, 1)
    image, gram_matrix = exchange(probes, fields, n_space, n_probe)
    count, planes, band, nz = image.shape
    norm_scale = math.sqrt(planes * band * nz * n_space * n_probe)
    basis_out, r_factor = basis(
        gram_matrix, image.reshape(count, planes * band, nz), norm_scale
    )
    return (basis_out.reshape(image.shape), r_factor)


def solution(mesh):
    placed = (
        P("probe", "space", None, None),
        P(None, None, "space", None, None),
        P("space"),
        P("space", None, None),
        P("space", None, None),
    )
    return jax.shard_map(
        per_device,
        mesh=mesh,
        in_specs=placed,
        out_specs=(P(None, "space", "probe", None), P()),
        check_vma=False,
    )
```

```python
import functools
import math

import jax
import jax.numpy as jnp
from jax import lax
from jax.experimental import pallas as pl
from jax.experimental.pallas import tpu as pltpu
from jax.sharding import PartitionSpec as P

diffusion = 0.1
MESH = pl.DeviceIdType.MESH
highest = lax.Precision.HIGHEST


def select_wind(winds, wind_step):
    levels = jnp.arange(winds.shape[0], dtype=jnp.int32)
    picked = levels[:, None] == wind_step[None, :]
    return jnp.sum(jnp.where(picked[:, None, :, None, None], winds, jnp.zeros_like(winds)), axis=0)


def exchange_kernel(
    n_space, n_probe, chunks, window,
    probes_ref, fields_ref, y_out, gram_out,
    field, fwd_state, coef, weighted, image, rows_ref, gram_acc, gram_part, reduce_buf, group_buf, total,
    own_sem, x_send, x_recv, zd_send, zf_send, lo_recv, hi_recv,
    f_own, f_xs, f_xr, f_zds, f_zfs, f_lor, f_hir, s_send, s_recv,
    a_send, a_recv, a_own, r_send, r_recv, g_send, g_recv, t_send, t_recv, y_sem,
):
    space = lax.axis_index("space")
    probe = lax.axis_index("probe")
    side = lax.rem(space, 2)
    partner = space + 1 - 2 * side
    group = lax.div(space, 2)
    n_group = n_space // 2
    base = space - side
    n_peer = 2 * n_probe
    mine = side * n_probe + probe
    half = probes_ref.shape[0] // 2
    per = half // chunks
    ny, nz = probes_ref.shape[2], probes_ref.shape[3]
    band = ny // n_probe
    below, above = space - 2, space + 2
    has_lo, has_hi = group > 0, group < n_group - 1

    def peer(step):
        other = lax.rem(mine + step, n_peer)
        return other, lax.div(other, n_probe), lax.rem(other, n_probe)

    def sister(step):
        other = lax.rem(group + step, n_group)
        return other, 2 * other + side

    barrier = pltpu.get_barrier_semaphore()
    for step in range(1, n_peer):
        _, px, pp = peer(step)
        pl.semaphore_signal(barrier, inc=1, device_id=(base + px, pp), device_id_type=MESH)
    for step in range(1, n_group):
        pl.semaphore_signal(
            barrier, inc=1, device_id=(sister(step)[1], probe), device_id_type=MESH
        )
    pl.semaphore_wait(barrier, n_peer + n_group - 2)

    def remote(src, dst, send, recv, dev):
        return pltpu.make_async_remote_copy(
            src_ref=src, dst_ref=dst, send_sem=send, recv_sem=recv,
            device_id=dev, device_id_type=MESH,
        )

    own_plane = 2 + 2 * side
    got_plane = 4 - 2 * side

    band_at = pl.ds(probe * band, band)
    own_f = pltpu.make_async_copy(fields_ref, field.at[pl.ds(1 + 2 * side, 2)], f_own)
    own_f.start()
    x_f = remote(
        fields_ref.at[:, :, band_at], field.at[pl.ds(1 + 2 * side, 2), :, band_at],
        f_xs, f_xr, (partner, probe),
    )
    x_f.start()

    def z_low(src, plane, send):
        return remote(
            src.at[plane, pl.ds(0, 4), band_at], field.at[5, pl.ds(0, 4), band_at],
            send, f_hir, (below, probe),
        )

    def z_high(src, plane, send):
        return remote(
            src.at[plane, pl.ds(0, 4), band_at], field.at[0, pl.ds(0, 4), band_at],
            send, f_lor, (above, probe),
        )

    def share_copy(kind, step):
        if kind == 0:
            ref = field.at[pl.ds(3 - 2 * side, 2), :, band_at]
        else:
            ref = field.at[0 if kind == 1 else 5, pl.ds(0, 4), band_at]
        to = lax.rem(probe + step, n_probe)
        return remote(
            ref, ref, s_send.at[kind, step], s_recv.at[kind, n_probe - step], (space, to)
        )

    def share_start(kind):
        for step in range(1, n_probe):
            share_copy(kind, step).start()

    def share_wait(kind):
        for step in range(1, n_probe):
            share_copy(kind, step).wait_recv()

    def share_drain(kind):
        for step in range(1, n_probe):
            share_copy(kind, step).wait_send()

    direct_lo = (side == 0) & has_lo
    direct_hi = (side == 1) & has_hi
    relay_hi = (side == 0) & has_hi
    relay_lo = (side == 1) & has_lo

    @pl.when(direct_lo)
    def _():
        z_low(fields_ref, 0, f_zds).start()

    @pl.when(direct_hi)
    def _():
        z_high(fields_ref, 1, f_zds).start()

    def chunk_at(c):
        return pl.ds(c * per, per)

    def x_copy(c):
        return remote(
            probes_ref.at[pl.ds((1 - side) * half + c * per, per)],
            fwd_state.at[chunk_at(c), pl.ds(own_plane, 2)],
            x_send.at[c], x_recv.at[c], (partner, probe),
        )

    def own_copy(c):
        return pltpu.make_async_copy(
            probes_ref.at[pl.ds(side * half + c * per, per)],
            fwd_state.at[chunk_at(c), pl.ds(own_plane, 2)],
            own_sem.at[c],
        )

    def zd_src(c):
        return probes_ref.at[pl.ds(side * half + c * per, per)]

    def zf_src(c):
        return fwd_state.at[chunk_at(c), pl.ds(got_plane, 2)]

    def lo_copy(src, c, send):
        return remote(
            src, fwd_state.at[chunk_at(c), pl.ds(6, 2)], send.at[c], hi_recv.at[c], (below, probe)
        )

    def hi_copy(src, c, send):
        return remote(
            src, fwd_state.at[chunk_at(c), pl.ds(0, 2)], send.at[c], lo_recv.at[c], (above, probe)
        )

    def launch(c):
        x_copy(c).start()
        own_copy(c).start()

        @pl.when(direct_lo)
        def _():
            lo_copy(zd_src(c), c, zd_send).start()

        @pl.when(direct_hi)
        def _():
            hi_copy(zd_src(c), c, zd_send).start()

    for c in range(window):
        launch(c)

    @pl.when(jnp.logical_not(has_lo))
    def _():
        field[0] = jnp.zeros(field.shape[1:], jnp.float32)

        def clear(i, carry):
            fwd_state[i, pl.ds(0, 2)] = jnp.zeros((2, ny, nz), jnp.float32)
            return carry

        lax.fori_loop(0, half, clear, 0)

    @pl.when(jnp.logical_not(has_hi))
    def _():
        field[5] = jnp.zeros(field.shape[1:], jnp.float32)

        def clear(i, carry):
            fwd_state[i, pl.ds(6, 2)] = jnp.zeros((2, ny, nz), jnp.float32)
            return carry

        lax.fori_loop(0, half, clear, 0)

    x_f.wait_recv()

    @pl.when(relay_hi)
    def _():
        z_high(field, 4, f_zfs).start()

    @pl.when(relay_lo)
    def _():
        z_low(field, 1, f_zfs).start()

    share_start(0)

    @pl.when(has_lo)
    def _():
        z_high(field, 0, f_zfs).wait_recv()
        share_start(1)

    @pl.when(has_hi)
    def _():
        z_low(field, 5, f_zfs).wait_recv()
        share_start(2)

    own_f.wait()
    share_wait(0)

    @pl.when(has_lo)
    def _():
        share_wait(1)

    @pl.when(has_hi)
    def _():
        share_wait(2)

    row_id = lax.broadcasted_iota(jnp.int32, (ny, nz), 0)
    col_id = lax.broadcasted_iota(jnp.int32, (ny, nz), 1)

    def make_coef(plane, carry):
        centre = jnp.full((ny, nz), 1.0 - 6.0 * diffusion, jnp.float32)
        for dim in range(3):
            speed = field[plane, dim]
            pos, neg = jnp.maximum(speed, 0.0), jnp.minimum(speed, 0.0)
            centre = centre - pos + neg
            up, down = pos + diffusion, diffusion - neg
            if dim == 1:
                up = jnp.where(row_id == 0, 0.0, up)
                down = jnp.where(row_id == ny - 1, 0.0, down)
            if dim == 2:
                up = jnp.where(col_id == 0, 0.0, up)
                down = jnp.where(col_id == nz - 1, 0.0, down)
            coef[plane, 1 + 2 * dim] = up
            coef[plane, 2 + 2 * dim] = down
        coef[plane, 0] = centre
        return carry

    lax.fori_loop(0, 6, make_coef, 0)

    def one_probe(i, carry):
        def tangent(plane, inner):
            u = fwd_state[i, plane + 1]
            out = coef[plane, 0] * u
            out += coef[plane, 1] * fwd_state[i, plane]
            out += coef[plane, 2] * fwd_state[i, plane + 2]
            out += coef[plane, 3] * pltpu.roll(u, 1, 0)
            out += coef[plane, 4] * pltpu.roll(u, ny - 1, 0)
            out += coef[plane, 5] * pltpu.roll(u, 1, 1)
            out += coef[plane, 6] * pltpu.roll(u, nz - 1, 1)
            weighted[plane] = field[plane, 3] * out
            return inner

        lax.fori_loop(0, 6, tangent, 0)

        def adjoint(at, inner):
            plane = at + 1
            v = weighted[plane]
            out = coef[plane, 0] * v + field[plane, 4] * fwd_state[i, plane + 1]
            out += coef[plane + 1, 1] * weighted[plane + 1]
            out += coef[plane - 1, 2] * weighted[plane - 1]
            out += pltpu.roll(coef[plane, 3] * v, ny - 1, 0)
            out += pltpu.roll(coef[plane, 4] * v, 1, 0)
            out += pltpu.roll(coef[plane, 5] * v, nz - 1, 1)
            out += pltpu.roll(coef[plane, 6] * v, 1, 1)
            image[i, at] = out
            return inner

        lax.fori_loop(0, 4, adjoint, 0)
        return carry

    def block_src(first, count, px, pp):
        return image.at[pl.ds(first, count), pl.ds(2 * px, 2), pl.ds(pp * band, band)]

    def block_dst(owner, first, count):
        return rows_ref.at[pl.ds(owner * half + first, count)]

    def rank_of(px, pp):
        return pp * 2 + px

    my_rank = rank_of(side, probe)

    def step_body(c, carry):
        @pl.when(c < chunks)
        def _():
            x_copy(c).wait_recv()

            @pl.when(relay_hi)
            def _():
                hi_copy(zf_src(c), c, zf_send).start()

            @pl.when(relay_lo)
            def _():
                lo_copy(zf_src(c), c, zf_send).start()

            @pl.when(c + window < chunks)
            def _():
                launch(c + window)

        @pl.when(c > 0)
        def _():
            d = c - 1
            own_copy(d).wait()

            @pl.when(has_lo)
            def _():
                hi_copy(zf_src(d), d, zf_send).wait_recv()

            @pl.when(has_hi)
            def _():
                lo_copy(zf_src(d), d, zf_send).wait_recv()

            lax.fori_loop(d * per, (d + 1) * per, one_probe, 0)
            for step in range(1, n_peer):
                _, px, pp = peer(step)
                remote(
                    block_src(d * per, per, px, pp), block_dst(my_rank, d * per, per),
                    a_send.at[step], a_recv.at[n_peer - step], (base + px, pp),
                ).start()
            pltpu.make_async_copy(
                block_src(d * per, per, side, probe), block_dst(my_rank, d * per, per), a_own
            ).start()

        return carry

    lax.fori_loop(0, chunks + 1, step_body, 0)

    for step in range(1, n_peer):
        _, px, pp = peer(step)
        remote(
            block_src(0, half, px, pp), block_dst(rank_of(px, pp), 0, half),
            a_send.at[step], a_recv.at[step], (base + px, pp),
        ).wait()
    pltpu.make_async_copy(
        block_src(0, half, side, probe), block_dst(my_rank, 0, half), a_own
    ).wait()

    y_copy = pltpu.make_async_copy(rows_ref, y_out, y_sem)
    y_copy.start()

    count = rows_ref.shape[0]
    depth = rows_ref.shape[1] * band
    flat = rows_ref.reshape(count * depth, nz)
    gram_acc[...] = jnp.zeros_like(gram_acc)

    def gram_step(t, carry):
        cols = jnp.concatenate(
            [flat[pl.ds(t * 8 + r, count, stride=depth), :] for r in range(8)], axis=1
        )
        both = jnp.concatenate(split(cols), axis=0)
        gram_acc[...] += lax.dot_general(
            both, both, (((1,), (1,)), ((), ())), preferred_element_type=jnp.float32
        )
        return carry

    lax.fori_loop(0, depth // 8, gram_step, 0)
    across = gram_acc[:count, count:] + gram_acc[count:, :count]
    gram_part[...] = gram_acc[:count, :count] + (across + gram_acc[count:, count:])

    share = count // n_peer

    def r_copy(step):
        other, px, pp = peer(step)
        return remote(
            gram_part.at[pl.ds(other * share, share)], reduce_buf.at[mine],
            r_send.at[step], r_recv.at[n_peer - step], (base + px, pp),
        )

    for step in range(1, n_peer):
        r_copy(step).start()
    reduce_buf[mine] = gram_part[pl.ds(pl.multiple_of(mine * share, share), share)]
    for step in range(1, n_peer):
        r_copy(step).wait_recv()
    group_buf[group] = jnp.sum(reduce_buf[...], axis=0)

    def g_copy(step):
        other, at = sister(step)
        return remote(
            group_buf.at[group], group_buf.at[group],
            g_send.at[step], g_recv.at[n_group - step], (at, probe),
        )

    for step in range(1, n_group):
        g_copy(step).start()
    for step in range(1, n_group):
        g_copy(step).wait_recv()
    total[pl.ds(pl.multiple_of(mine * share, share), share)] = jnp.sum(group_buf[...], axis=0)

    def t_copy(step):
        _, px, pp = peer(step)
        return remote(
            total.at[pl.ds(mine * share, share)], total.at[pl.ds(mine * share, share)],
            t_send.at[step], t_recv.at[n_peer - step], (base + px, pp),
        )

    for step in range(1, n_peer):
        t_copy(step).start()
    for step in range(1, n_peer):
        t_copy(step).wait_recv()
    gram_out[...] = total[...]

    for step in range(1, n_peer):
        r_copy(step).wait_send()
        t_copy(step).wait_send()
    for step in range(1, n_group):
        g_copy(step).wait_send()
    x_f.wait_send()
    share_drain(0)

    @pl.when(has_lo)
    def _():
        share_drain(1)

    @pl.when(has_hi)
    def _():
        share_drain(2)

    @pl.when(direct_lo)
    def _():
        z_low(fields_ref, 0, f_zds).wait_send()

    @pl.when(direct_hi)
    def _():
        z_high(fields_ref, 1, f_zds).wait_send()

    @pl.when(relay_hi)
    def _():
        z_high(field, 4, f_zfs).wait_send()

    @pl.when(relay_lo)
    def _():
        z_low(field, 1, f_zfs).wait_send()

    def drain(c, carry):
        x_copy(c).wait_send()

        @pl.when(direct_lo)
        def _():
            lo_copy(zd_src(c), c, zd_send).wait_send()

        @pl.when(direct_hi)
        def _():
            hi_copy(zd_src(c), c, zd_send).wait_send()

        @pl.when(relay_hi)
        def _():
            hi_copy(zf_src(c), c, zf_send).wait_send()

        @pl.when(relay_lo)
        def _():
            lo_copy(zf_src(c), c, zf_send).wait_send()

        return carry

    lax.fori_loop(0, chunks, drain, 0)
    y_copy.wait()


def exchange(probes, fields, n_space, n_probe, chunks=8, window=8):
    local, planes, ny, nz = probes.shape
    count = local * n_probe
    half = local // 2
    band = ny // n_probe
    n_peer, n_group = 2 * n_probe, n_space // 2
    share = count // n_peer
    f32 = jnp.float32
    dma = pltpu.SemaphoreType.DMA
    return pl.pallas_call(
        functools.partial(exchange_kernel, n_space, n_probe, chunks, window),
        out_shape=(
            jax.ShapeDtypeStruct((count, planes, band, nz), f32),
            jax.ShapeDtypeStruct((count, count), f32),
        ),
        in_specs=[pl.BlockSpec(memory_space=pl.ANY)] * 2,
        out_specs=(
            pl.BlockSpec(memory_space=pl.ANY),
            pl.BlockSpec(memory_space=pltpu.VMEM),
        ),
        scratch_shapes=[
            pltpu.VMEM((6, 5, ny, nz), f32),
            pltpu.VMEM((half, 8, ny, nz), f32),
            pltpu.VMEM((6, 7, ny, nz), f32),
            pltpu.VMEM((6, ny, nz), f32),
            pltpu.VMEM((half, 4, ny, nz), f32),
            pltpu.VMEM((count, planes, band, nz), f32),
            pltpu.VMEM((2 * count, 2 * count), f32),
            pltpu.VMEM((count, count), f32),
            pltpu.VMEM((n_peer, share, count), f32),
            pltpu.VMEM((n_group, share, count), f32),
            pltpu.VMEM((count, count), f32),
        ]
        + [dma((chunks,))] * 7
        + [dma(())] * 7
        + [dma((3, n_probe))] * 2
        + [dma((n_peer,)), dma((n_peer,)), dma(())]
        + [dma((n_peer,)), dma((n_peer,)), dma((n_group,)), dma((n_group,))]
        + [dma((n_peer,)), dma((n_peer,)), dma(())],
        compiler_params=pltpu.CompilerParams(
            collective_id=0, has_side_effects=True, vmem_limit_bytes=32 * 1024 * 1024
        ),
        name="exchange",
    )(probes, fields)


def split(values):
    high = values.astype(jnp.bfloat16)
    low = (values - high.astype(jnp.float32)).astype(jnp.bfloat16)
    return high, low


def terms(values):
    found = []
    for _ in range(3):
        found.append(values.astype(jnp.bfloat16).astype(jnp.float32))
        values = values - found[-1]
    return found


def factor(gram_ref, work, n, rows=8):
    work[:, :n] = gram_ref[...]
    row_id = lax.broadcasted_iota(jnp.int32, (n, n), 0)
    col_id = lax.broadcasted_iota(jnp.int32, (n, n), 1)
    work[:, n:] = jnp.where(row_id == col_id, 1.0, 0.0)
    sub = lax.broadcasted_iota(jnp.int32, (rows, n), 0)
    lane = lax.broadcasted_iota(jnp.int32, (rows, n), 1)

    def panel_step(at, carry):
        start = pl.multiple_of(at * rows, rows)
        left = pltpu.roll(work[pl.ds(start, rows), :n], lax.rem(n - start, n), 1)
        right = work[pl.ds(start, rows), n:]
        columns = [jnp.broadcast_to(left[:, j : j + 1], (rows, n)) for j in range(rows)]
        pivots = columns[0]
        for j in range(rows):
            pivot = jnp.broadcast_to(columns[j][j : j + 1, :], (rows, n))
            times = jnp.where(sub > j, columns[j] * (1.0 / pivot), 0.0)
            pivots = jnp.where(sub == j, pivot, pivots)
            if j == rows - 1:
                break
            for i in range(j + 1, rows):
                columns[i] -= times * jnp.broadcast_to(columns[i][j : j + 1, :], (rows, n))
            left -= times * jnp.broadcast_to(left[j : j + 1, :], (rows, n))
            right -= times * jnp.broadcast_to(right[j : j + 1, :], (rows, n))
        scale = lax.rsqrt(pivots)
        scale = scale * (1.5 - 0.5 * (pivots * scale) * scale)
        left = pltpu.roll(left * scale, start, 1)
        right = right * scale
        ahead = jnp.where(lane >= start + rows, left, 0.0)
        both = jnp.concatenate([left, right], axis=1)
        a_terms, b_terms = terms(ahead), terms(both)
        pairs = ((0, 0), (0, 1), (1, 0), (1, 1), (0, 2), (2, 0))
        stacked_a = jnp.concatenate([a_terms[i] for i, _ in pairs], axis=0)
        stacked_b = jnp.concatenate([b_terms[i] for _, i in pairs], axis=0)
        work[...] -= lax.dot_general(
            stacked_a.astype(jnp.bfloat16), stacked_b.astype(jnp.bfloat16),
            (((0,), (0,)), ((), ())), preferred_element_type=jnp.float32,
        )
        work[pl.ds(start, rows), :] = both
        return carry

    lax.fori_loop(0, n // rows, panel_step, 0)
    upper = jnp.where(row_id <= col_id, work[:, :n], 0.0)
    return upper, work[:, n:]


def basis_kernel(
    norm_scale, gram_ref, y_ref, out_hbm, factor_ref, work, out_ref, out_sem
):
    count, depth, nz = y_ref.shape
    upper, inverse = factor(gram_ref, work, count)
    factor_ref[...] = upper / norm_scale
    high, low = split(inverse * norm_scale)
    left = jnp.concatenate([high, low, high, low], axis=1)
    flat = y_ref.reshape(count * depth, nz)
    result_flat = out_ref.reshape(count * depth, nz)
    rows = 8

    def store(t):
        part = pl.ds(pl.multiple_of(t * rows, rows), rows)
        return pltpu.make_async_copy(out_ref.at[:, part], out_hbm.at[:, part], out_sem.at[t])

    def block_step(t, carry):
        cols = jnp.concatenate(
            [flat[pl.ds(t * rows + r, count, stride=depth), :] for r in range(rows)], axis=1
        )
        y_high, y_low = split(cols)
        right = jnp.concatenate([y_high, y_high, y_low, y_low], axis=0)
        result = jnp.dot(left, right, preferred_element_type=jnp.float32)
        for r in range(rows):
            result_flat[pl.ds(t * rows + r, count, stride=depth), :] = result[
                :, r * nz : (r + 1) * nz
            ]
        store(t).start()
        return carry

    lax.fori_loop(0, depth // rows, block_step, 0)

    def drain(t, carry):
        store(t).wait()
        return carry

    lax.fori_loop(0, depth // rows, drain, 0)


def basis(gram_matrix, y_rows, norm_scale):
    count, depth, nz = y_rows.shape
    f32 = jnp.float32
    vmem = pl.BlockSpec(memory_space=pltpu.VMEM)
    hbm = pl.BlockSpec(memory_space=pl.ANY)
    return pl.pallas_call(
        functools.partial(basis_kernel, norm_scale),
        out_shape=(
            jax.ShapeDtypeStruct(y_rows.shape, f32),
            jax.ShapeDtypeStruct(gram_matrix.shape, f32),
        ),
        in_specs=[vmem, vmem],
        out_specs=(hbm, vmem),
        scratch_shapes=[
            pltpu.VMEM((count, 2 * count), f32),
            pltpu.VMEM(y_rows.shape, f32),
            pltpu.SemaphoreType.DMA((depth // 8,)),
        ],
        compiler_params=pltpu.CompilerParams(vmem_limit_bytes=24 * 1024 * 1024),
        name="basis",
    )(gram_matrix, y_rows)


def per_device(probes, winds, wind_step, obs_weight, prior_weight):
    n_space, n_probe = lax.axis_size("space"), lax.axis_size("probe")
    wind_now = select_wind(winds, wind_step)
    fields = jnp.concatenate([wind_now, obs_weight[None], prior_weight[None]], axis=0)
    fields = jnp.swapaxes(fields, 0, 1)
    image, gram_matrix = exchange(probes, fields, n_space, n_probe)
    count, planes, band, nz = image.shape
    norm_scale = math.sqrt(planes * band * nz * n_space * n_probe)
    basis_out, r_factor = basis(
        gram_matrix, image.reshape(count, planes * band, nz), norm_scale
    )
    return (basis_out.reshape(image.shape), r_factor)


def solution(mesh):
    placed = (
        P("probe", "space", None, None),
        P(None, None, "space", None, None),
        P("space"),
        P("space", None, None),
        P("space", None, None),
    )
    return jax.shard_map(
        per_device,
        mesh=mesh,
        in_specs=placed,
        out_specs=(P(None, "space", "probe", None), P()),
        check_vma=False,
    )
```

```python
import functools
import math

import jax
import jax.numpy as jnp
from jax import lax
from jax.experimental import pallas as pl
from jax.experimental.pallas import tpu as pltpu
from jax.sharding import PartitionSpec as P

diffusion = 0.1
MESH = pl.DeviceIdType.MESH
highest = lax.Precision.HIGHEST


def select_wind(winds, wind_step):
    levels = jnp.arange(winds.shape[0], dtype=jnp.int32)
    picked = levels[:, None] == wind_step[None, :]
    return jnp.sum(jnp.where(picked[:, None, :, None, None], winds, jnp.zeros_like(winds)), axis=0)


def exchange_kernel(
    n_space, n_probe, chunks, window,
    probes_ref, fields_ref, y_out, gram_out,
    field, fwd_state, coef, weighted, image, rows_ref, gram_acc, gram_part, reduce_buf, group_buf, total,
    own_sem, x_send, x_recv, zd_send, zf_send, lo_recv, hi_recv,
    f_own, f_xs, f_xr, f_zds, f_zfs, f_lor, f_hir, s_send, s_recv,
    a_send, a_recv, a_own, r_send, r_recv, g_send, g_recv, t_send, t_recv, y_sem,
):
    space = lax.axis_index("space")
    probe = lax.axis_index("probe")
    side = lax.rem(space, 2)
    partner = space + 1 - 2 * side
    group = lax.div(space, 2)
    n_group = n_space // 2
    base = space - side
    n_peer = 2 * n_probe
    mine = side * n_probe + probe
    half = probes_ref.shape[0] // 2
    per = half // chunks
    ny, nz = probes_ref.shape[2], probes_ref.shape[3]
    band = ny // n_probe
    below, above = space - 2, space + 2
    has_lo, has_hi = group > 0, group < n_group - 1

    def peer(step):
        other = lax.rem(mine + step, n_peer)
        return other, lax.div(other, n_probe), lax.rem(other, n_probe)

    def sister(step):
        other = lax.rem(group + step, n_group)
        return other, 2 * other + side

    barrier = pltpu.get_barrier_semaphore()
    for step in range(1, n_peer):
        _, px, pp = peer(step)
        pl.semaphore_signal(barrier, inc=1, device_id=(base + px, pp), device_id_type=MESH)
    for step in range(1, n_group):
        pl.semaphore_signal(
            barrier, inc=1, device_id=(sister(step)[1], probe), device_id_type=MESH
        )
    pl.semaphore_wait(barrier, n_peer + n_group - 2)

    def remote(src, dst, send, recv, dev):
        return pltpu.make_async_remote_copy(
            src_ref=src, dst_ref=dst, send_sem=send, recv_sem=recv,
            device_id=dev, device_id_type=MESH,
        )

    own_plane = 2 + 2 * side
    got_plane = 4 - 2 * side

    band_at = pl.ds(probe * band, band)
    own_f = pltpu.make_async_copy(fields_ref, field.at[pl.ds(1 + 2 * side, 2)], f_own)
    own_f.start()
    x_f = remote(
        fields_ref.at[:, :, band_at], field.at[pl.ds(1 + 2 * side, 2), :, band_at],
        f_xs, f_xr, (partner, probe),
    )
    x_f.start()

    def z_low(src, plane, send):
        return remote(
            src.at[plane, pl.ds(0, 4), band_at], field.at[5, pl.ds(0, 4), band_at],
            send, f_hir, (below, probe),
        )

    def z_high(src, plane, send):
        return remote(
            src.at[plane, pl.ds(0, 4), band_at], field.at[0, pl.ds(0, 4), band_at],
            send, f_lor, (above, probe),
        )

    def share_copy(kind, step):
        if kind == 0:
            ref = field.at[pl.ds(3 - 2 * side, 2), :, band_at]
        else:
            ref = field.at[0 if kind == 1 else 5, pl.ds(0, 4), band_at]
        to = lax.rem(probe + step, n_probe)
        return remote(
            ref, ref, s_send.at[kind, step], s_recv.at[kind, n_probe - step], (space, to)
        )

    def share_start(kind):
        for step in range(1, n_probe):
            share_copy(kind, step).start()

    def share_wait(kind):
        for step in range(1, n_probe):
            share_copy(kind, step).wait_recv()

    def share_drain(kind):
        for step in range(1, n_probe):
            share_copy(kind, step).wait_send()

    direct_lo = (side == 0) & has_lo
    direct_hi = (side == 1) & has_hi
    relay_hi = (side == 0) & has_hi
    relay_lo = (side == 1) & has_lo

    @pl.when(direct_lo)
    def _():
        z_low(fields_ref, 0, f_zds).start()

    @pl.when(direct_hi)
    def _():
        z_high(fields_ref, 1, f_zds).start()

    def chunk_at(c):
        return pl.ds(c * per, per)

    def x_copy(c):
        return remote(
            probes_ref.at[pl.ds((1 - side) * half + c * per, per)],
            fwd_state.at[chunk_at(c), pl.ds(own_plane, 2)],
            x_send.at[c], x_recv.at[c], (partner, probe),
        )

    def own_copy(c):
        return pltpu.make_async_copy(
            probes_ref.at[pl.ds(side * half + c * per, per)],
            fwd_state.at[chunk_at(c), pl.ds(own_plane, 2)],
            own_sem.at[c],
        )

    def zd_src(c):
        return probes_ref.at[pl.ds(side * half + c * per, per)]

    def zf_src(c):
        return fwd_state.at[chunk_at(c), pl.ds(got_plane, 2)]

    def lo_copy(src, c, send):
        return remote(
            src, fwd_state.at[chunk_at(c), pl.ds(6, 2)], send.at[c], hi_recv.at[c], (below, probe)
        )

    def hi_copy(src, c, send):
        return remote(
            src, fwd_state.at[chunk_at(c), pl.ds(0, 2)], send.at[c], lo_recv.at[c], (above, probe)
        )

    def launch(c):
        x_copy(c).start()
        own_copy(c).start()

        @pl.when(direct_lo)
        def _():
            lo_copy(zd_src(c), c, zd_send).start()

        @pl.when(direct_hi)
        def _():
            hi_copy(zd_src(c), c, zd_send).start()

    for c in range(window):
        launch(c)

    @pl.when(jnp.logical_not(has_lo))
    def _():
        field[0] = jnp.zeros(field.shape[1:], jnp.float32)

        def clear(i, carry):
            fwd_state[i, pl.ds(0, 2)] = jnp.zeros((2, ny, nz), jnp.float32)
            return carry

        lax.fori_loop(0, half, clear, 0)

    @pl.when(jnp.logical_not(has_hi))
    def _():
        field[5] = jnp.zeros(field.shape[1:], jnp.float32)

        def clear(i, carry):
            fwd_state[i, pl.ds(6, 2)] = jnp.zeros((2, ny, nz), jnp.float32)
            return carry

        lax.fori_loop(0, half, clear, 0)

    x_f.wait_recv()

    @pl.when(relay_hi)
    def _():
        z_high(field, 4, f_zfs).start()

    @pl.when(relay_lo)
    def _():
        z_low(field, 1, f_zfs).start()

    share_start(0)

    @pl.when(has_lo)
    def _():
        z_high(field, 0, f_zfs).wait_recv()
        share_start(1)

    @pl.when(has_hi)
    def _():
        z_low(field, 5, f_zfs).wait_recv()
        share_start(2)

    own_f.wait()
    share_wait(0)

    @pl.when(has_lo)
    def _():
        share_wait(1)

    @pl.when(has_hi)
    def _():
        share_wait(2)

    row_id = lax.broadcasted_iota(jnp.int32, (ny, nz), 0)
    col_id = lax.broadcasted_iota(jnp.int32, (ny, nz), 1)

    def make_coef(plane, carry):
        centre = jnp.full((ny, nz), 1.0 - 6.0 * diffusion, jnp.float32)
        for dim in range(3):
            speed = field[plane, dim]
            pos, neg = jnp.maximum(speed, 0.0), jnp.minimum(speed, 0.0)
            centre = centre - pos + neg
            up, down = pos + diffusion, diffusion - neg
            if dim == 1:
                up = jnp.where(row_id == 0, 0.0, up)
                down = jnp.where(row_id == ny - 1, 0.0, down)
            if dim == 2:
                up = jnp.where(col_id == 0, 0.0, up)
                down = jnp.where(col_id == nz - 1, 0.0, down)
            coef[plane, 1 + 2 * dim] = up
            coef[plane, 2 + 2 * dim] = down
        coef[plane, 0] = centre
        return carry

    lax.fori_loop(0, 6, make_coef, 0)

    def one_probe(i, carry):
        def tangent(plane, inner):
            u = fwd_state[i, plane + 1]
            out = coef[plane, 0] * u
            out += coef[plane, 1] * fwd_state[i, plane]
            out += coef[plane, 2] * fwd_state[i, plane + 2]
            out += coef[plane, 3] * pltpu.roll(u, 1, 0)
            out += coef[plane, 4] * pltpu.roll(u, ny - 1, 0)
            out += coef[plane, 5] * pltpu.roll(u, 1, 1)
            out += coef[plane, 6] * pltpu.roll(u, nz - 1, 1)
            weighted[plane] = field[plane, 3] * out
            return inner

        lax.fori_loop(0, 6, tangent, 0)

        def adjoint(at, inner):
            plane = at + 1
            v = weighted[plane]
            out = coef[plane, 0] * v + field[plane, 4] * fwd_state[i, plane + 1]
            out += coef[plane + 1, 1] * weighted[plane + 1]
            out += coef[plane - 1, 2] * weighted[plane - 1]
            out += pltpu.roll(coef[plane, 3] * v, ny - 1, 0)
            out += pltpu.roll(coef[plane, 4] * v, 1, 0)
            out += pltpu.roll(coef[plane, 5] * v, nz - 1, 1)
            out += pltpu.roll(coef[plane, 6] * v, 1, 1)
            image[i, at] = out
            return inner

        lax.fori_loop(0, 4, adjoint, 0)
        return carry

    def block_src(first, count, px, pp):
        return image.at[pl.ds(first, count), pl.ds(2 * px, 2), pl.ds(pp * band, band)]

    def block_dst(owner, first, count):
        return rows_ref.at[pl.ds(owner * half + first, count)]

    def rank_of(px, pp):
        return pp * 2 + px

    my_rank = rank_of(side, probe)

    def step_body(c, carry):
        @pl.when(c < chunks)
        def _():
            x_copy(c).wait_recv()

            @pl.when(relay_hi)
            def _():
                hi_copy(zf_src(c), c, zf_send).start()

            @pl.when(relay_lo)
            def _():
                lo_copy(zf_src(c), c, zf_send).start()

            @pl.when(c + window < chunks)
            def _():
                launch(c + window)

        @pl.when(c > 0)
        def _():
            d = c - 1
            own_copy(d).wait()

            @pl.when(has_lo)
            def _():
                hi_copy(zf_src(d), d, zf_send).wait_recv()

            @pl.when(has_hi)
            def _():
                lo_copy(zf_src(d), d, zf_send).wait_recv()

            lax.fori_loop(d * per, (d + 1) * per, one_probe, 0)
            for step in range(1, n_peer):
                _, px, pp = peer(step)
                remote(
                    block_src(d * per, per, px, pp), block_dst(my_rank, d * per, per),
                    a_send.at[step], a_recv.at[n_peer - step], (base + px, pp),
                ).start()
            pltpu.make_async_copy(
                block_src(d * per, per, side, probe), block_dst(my_rank, d * per, per), a_own
            ).start()

        return carry

    lax.fori_loop(0, chunks + 1, step_body, 0)

    for step in range(1, n_peer):
        _, px, pp = peer(step)
        remote(
            block_src(0, half, px, pp), block_dst(rank_of(px, pp), 0, half),
            a_send.at[step], a_recv.at[step], (base + px, pp),
        ).wait()
    pltpu.make_async_copy(
        block_src(0, half, side, probe), block_dst(my_rank, 0, half), a_own
    ).wait()

    y_copy = pltpu.make_async_copy(rows_ref, y_out, y_sem)
    y_copy.start()

    count = rows_ref.shape[0]
    depth = rows_ref.shape[1] * band
    flat = rows_ref.reshape(count * depth, nz)
    gram_acc[...] = jnp.zeros_like(gram_acc)

    def gram_step(t, carry):
        cols = jnp.concatenate(
            [flat[pl.ds(t * 8 + r, count, stride=depth), :] for r in range(8)], axis=1
        )
        both = jnp.concatenate(split(cols), axis=0)
        gram_acc[...] += lax.dot_general(
            both, both, (((1,), (1,)), ((), ())), preferred_element_type=jnp.float32
        )
        return carry

    lax.fori_loop(0, depth // 8, gram_step, 0)
    across = gram_acc[:count, count:] + gram_acc[count:, :count]
    gram_part[...] = gram_acc[:count, :count] + (across + gram_acc[count:, count:])

    share = count // n_peer

    def r_copy(step):
        other, px, pp = peer(step)
        return remote(
            gram_part.at[pl.ds(other * share, share)], reduce_buf.at[mine],
            r_send.at[step], r_recv.at[n_peer - step], (base + px, pp),
        )

    for step in range(1, n_peer):
        r_copy(step).start()
    reduce_buf[mine] = gram_part[pl.ds(pl.multiple_of(mine * share, share), share)]
    for step in range(1, n_peer):
        r_copy(step).wait_recv()
    group_buf[group] = jnp.sum(reduce_buf[...], axis=0)

    def g_copy(step):
        other, at = sister(step)
        return remote(
            group_buf.at[group], group_buf.at[group],
            g_send.at[step], g_recv.at[n_group - step], (at, probe),
        )

    for step in range(1, n_group):
        g_copy(step).start()
    for step in range(1, n_group):
        g_copy(step).wait_recv()
    total[pl.ds(pl.multiple_of(mine * share, share), share)] = jnp.sum(group_buf[...], axis=0)

    def t_copy(step):
        _, px, pp = peer(step)
        return remote(
            total.at[pl.ds(mine * share, share)], total.at[pl.ds(mine * share, share)],
            t_send.at[step], t_recv.at[n_peer - step], (base + px, pp),
        )

    for step in range(1, n_peer):
        t_copy(step).start()
    for step in range(1, n_peer):
        t_copy(step).wait_recv()
    gram_out[...] = total[...]

    for step in range(1, n_peer):
        r_copy(step).wait_send()
        t_copy(step).wait_send()
    for step in range(1, n_group):
        g_copy(step).wait_send()
    x_f.wait_send()
    share_drain(0)

    @pl.when(has_lo)
    def _():
        share_drain(1)

    @pl.when(has_hi)
    def _():
        share_drain(2)

    @pl.when(direct_lo)
    def _():
        z_low(fields_ref, 0, f_zds).wait_send()

    @pl.when(direct_hi)
    def _():
        z_high(fields_ref, 1, f_zds).wait_send()

    @pl.when(relay_hi)
    def _():
        z_high(field, 4, f_zfs).wait_send()

    @pl.when(relay_lo)
    def _():
        z_low(field, 1, f_zfs).wait_send()

    def drain(c, carry):
        x_copy(c).wait_send()

        @pl.when(direct_lo)
        def _():
            lo_copy(zd_src(c), c, zd_send).wait_send()

        @pl.when(direct_hi)
        def _():
            hi_copy(zd_src(c), c, zd_send).wait_send()

        @pl.when(relay_hi)
        def _():
            hi_copy(zf_src(c), c, zf_send).wait_send()

        @pl.when(relay_lo)
        def _():
            lo_copy(zf_src(c), c, zf_send).wait_send()

        return carry

    lax.fori_loop(0, chunks, drain, 0)
    y_copy.wait()


def exchange(probes, fields, n_space, n_probe, chunks=4, window=4):
    local, planes, ny, nz = probes.shape
    count = local * n_probe
    half = local // 2
    band = ny // n_probe
    n_peer, n_group = 2 * n_probe, n_space // 2
    share = count // n_peer
    f32 = jnp.float32
    dma = pltpu.SemaphoreType.DMA
    return pl.pallas_call(
        functools.partial(exchange_kernel, n_space, n_probe, chunks, window),
        out_shape=(
            jax.ShapeDtypeStruct((count, planes, band, nz), f32),
            jax.ShapeDtypeStruct((count, count), f32),
        ),
        in_specs=[pl.BlockSpec(memory_space=pl.ANY)] * 2,
        out_specs=(
            pl.BlockSpec(memory_space=pl.ANY),
            pl.BlockSpec(memory_space=pltpu.VMEM),
        ),
        scratch_shapes=[
            pltpu.VMEM((6, 5, ny, nz), f32),
            pltpu.VMEM((half, 8, ny, nz), f32),
            pltpu.VMEM((6, 7, ny, nz), f32),
            pltpu.VMEM((6, ny, nz), f32),
            pltpu.VMEM((half, 4, ny, nz), f32),
            pltpu.VMEM((count, planes, band, nz), f32),
            pltpu.VMEM((2 * count, 2 * count), f32),
            pltpu.VMEM((count, count), f32),
            pltpu.VMEM((n_peer, share, count), f32),
            pltpu.VMEM((n_group, share, count), f32),
            pltpu.VMEM((count, count), f32),
        ]
        + [dma((chunks,))] * 7
        + [dma(())] * 7
        + [dma((3, n_probe))] * 2
        + [dma((n_peer,)), dma((n_peer,)), dma(())]
        + [dma((n_peer,)), dma((n_peer,)), dma((n_group,)), dma((n_group,))]
        + [dma((n_peer,)), dma((n_peer,)), dma(())],
        compiler_params=pltpu.CompilerParams(
            collective_id=0, has_side_effects=True, vmem_limit_bytes=48 * 1024 * 1024
        ),
        name="exchange",
    )(probes, fields)


def split(values):
    high = values.astype(jnp.bfloat16)
    low = (values - high.astype(jnp.float32)).astype(jnp.bfloat16)
    return high, low


def terms(values):
    found = []
    for _ in range(3):
        found.append(values.astype(jnp.bfloat16).astype(jnp.float32))
        values = values - found[-1]
    return found


def factor(gram_ref, work, n, rows=8):
    work[:, :n] = gram_ref[...]
    row_id = lax.broadcasted_iota(jnp.int32, (n, n), 0)
    col_id = lax.broadcasted_iota(jnp.int32, (n, n), 1)
    work[:, n:] = jnp.where(row_id == col_id, 1.0, 0.0)
    sub = lax.broadcasted_iota(jnp.int32, (rows, n), 0)
    lane = lax.broadcasted_iota(jnp.int32, (rows, n), 1)

    def panel_step(at, carry):
        start = pl.multiple_of(at * rows, rows)
        left = pltpu.roll(work[pl.ds(start, rows), :n], lax.rem(n - start, n), 1)
        right = work[pl.ds(start, rows), n:]
        columns = [jnp.broadcast_to(left[:, j : j + 1], (rows, n)) for j in range(rows)]
        pivots = columns[0]
        for j in range(rows):
            pivot = jnp.broadcast_to(columns[j][j : j + 1, :], (rows, n))
            times = jnp.where(sub > j, columns[j] * (1.0 / pivot), 0.0)
            pivots = jnp.where(sub == j, pivot, pivots)
            if j == rows - 1:
                break
            for i in range(j + 1, rows):
                columns[i] -= times * jnp.broadcast_to(columns[i][j : j + 1, :], (rows, n))
            left -= times * jnp.broadcast_to(left[j : j + 1, :], (rows, n))
            right -= times * jnp.broadcast_to(right[j : j + 1, :], (rows, n))
        scale = lax.rsqrt(pivots)
        scale = scale * (1.5 - 0.5 * (pivots * scale) * scale)
        left = pltpu.roll(left * scale, start, 1)
        right = right * scale
        ahead = jnp.where(lane >= start + rows, left, 0.0)
        both = jnp.concatenate([left, right], axis=1)
        a_terms, b_terms = terms(ahead), terms(both)
        pairs = ((0, 0), (0, 1), (1, 0), (1, 1), (0, 2), (2, 0))
        stacked_a = jnp.concatenate([a_terms[i] for i, _ in pairs], axis=0)
        stacked_b = jnp.concatenate([b_terms[i] for _, i in pairs], axis=0)
        work[...] -= lax.dot_general(
            stacked_a.astype(jnp.bfloat16), stacked_b.astype(jnp.bfloat16),
            (((0,), (0,)), ((), ())), preferred_element_type=jnp.float32,
        )
        work[pl.ds(start, rows), :] = both
        return carry

    lax.fori_loop(0, n // rows, panel_step, 0)
    upper = jnp.where(row_id <= col_id, work[:, :n], 0.0)
    return upper, work[:, n:]


def basis_kernel(
    norm_scale, gram_ref, y_ref, out_hbm, factor_ref, work, out_ref, out_sem
):
    count, depth, nz = y_ref.shape
    upper, inverse = factor(gram_ref, work, count)
    factor_ref[...] = upper / norm_scale
    high, low = split(inverse * norm_scale)
    left = jnp.concatenate([high, low, high, low], axis=1)
    flat = y_ref.reshape(count * depth, nz)
    result_flat = out_ref.reshape(count * depth, nz)
    rows = 8

    def store(t):
        part = pl.ds(pl.multiple_of(t * rows, rows), rows)
        return pltpu.make_async_copy(out_ref.at[:, part], out_hbm.at[:, part], out_sem.at[t])

    def block_step(t, carry):
        cols = jnp.concatenate(
            [flat[pl.ds(t * rows + r, count, stride=depth), :] for r in range(rows)], axis=1
        )
        y_high, y_low = split(cols)
        right = jnp.concatenate([y_high, y_high, y_low, y_low], axis=0)
        result = jnp.dot(left, right, preferred_element_type=jnp.float32)
        for r in range(rows):
            result_flat[pl.ds(t * rows + r, count, stride=depth), :] = result[
                :, r * nz : (r + 1) * nz
            ]
        store(t).start()
        return carry

    lax.fori_loop(0, depth // rows, block_step, 0)

    def drain(t, carry):
        store(t).wait()
        return carry

    lax.fori_loop(0, depth // rows, drain, 0)


def basis(gram_matrix, y_rows, norm_scale):
    count, depth, nz = y_rows.shape
    f32 = jnp.float32
    vmem = pl.BlockSpec(memory_space=pltpu.VMEM)
    hbm = pl.BlockSpec(memory_space=pl.ANY)
    return pl.pallas_call(
        functools.partial(basis_kernel, norm_scale),
        out_shape=(
            jax.ShapeDtypeStruct(y_rows.shape, f32),
            jax.ShapeDtypeStruct(gram_matrix.shape, f32),
        ),
        in_specs=[vmem, vmem],
        out_specs=(hbm, vmem),
        scratch_shapes=[
            pltpu.VMEM((count, 2 * count), f32),
            pltpu.VMEM(y_rows.shape, f32),
            pltpu.SemaphoreType.DMA((depth // 8,)),
        ],
        compiler_params=pltpu.CompilerParams(vmem_limit_bytes=24 * 1024 * 1024),
        name="basis",
    )(gram_matrix, y_rows)


def per_device(probes, winds, wind_step, obs_weight, prior_weight):
    n_space, n_probe = lax.axis_size("space"), lax.axis_size("probe")
    wind_now = select_wind(winds, wind_step)
    fields = jnp.concatenate([wind_now, obs_weight[None], prior_weight[None]], axis=0)
    fields = jnp.swapaxes(fields, 0, 1)
    image, gram_matrix = exchange(probes, fields, n_space, n_probe)
    count, planes, band, nz = image.shape
    norm_scale = math.sqrt(planes * band * nz * n_space * n_probe)
    basis_out, r_factor = basis(
        gram_matrix, image.reshape(count, planes * band, nz), norm_scale
    )
    return (basis_out.reshape(image.shape), r_factor)


def solution(mesh):
    placed = (
        P("probe", "space", None, None),
        P(None, None, "space", None, None),
        P("space"),
        P("space", None, None),
        P("space", None, None),
    )
    return jax.shard_map(
        per_device,
        mesh=mesh,
        in_specs=placed,
        out_specs=(P(None, "space", "probe", None), P()),
        check_vma=False,
    )
```

```python
import functools
import math

import jax
import jax.numpy as jnp
from jax import lax
from jax.experimental import pallas as pl
from jax.experimental.pallas import tpu as pltpu
from jax.sharding import PartitionSpec as P

diffusion = 0.1
MESH = pl.DeviceIdType.MESH
highest = lax.Precision.HIGHEST


def select_wind(winds, wind_step):
    levels = jnp.arange(winds.shape[0], dtype=jnp.int32)
    picked = levels[:, None] == wind_step[None, :]
    return jnp.sum(jnp.where(picked[:, None, :, None, None], winds, jnp.zeros_like(winds)), axis=0)


def exchange_kernel(
    n_space, n_probe, chunks, window,
    probes_ref, fields_ref, y_out, gram_out,
    field, fwd_state, coef, weighted, image, rows_ref, gram_acc, gram_part, reduce_buf, group_buf, total,
    own_sem, x_send, x_recv, zd_send, zf_send, lo_recv, hi_recv,
    f_own, f_xs, f_xr, f_zds, f_zfs, f_lor, f_hir, s_send, s_recv,
    a_send, a_recv, a_own, r_send, r_recv, g_send, g_recv, t_send, t_recv, y_sem,
):
    space = lax.axis_index("space")
    probe = lax.axis_index("probe")
    side = lax.rem(space, 2)
    partner = space + 1 - 2 * side
    group = lax.div(space, 2)
    n_group = n_space // 2
    base = space - side
    n_peer = 2 * n_probe
    mine = side * n_probe + probe
    half = probes_ref.shape[0] // 2
    per = half // chunks
    ny, nz = probes_ref.shape[2], probes_ref.shape[3]
    band = ny // n_probe
    below, above = space - 2, space + 2
    has_lo, has_hi = group > 0, group < n_group - 1

    def peer(step):
        other = lax.rem(mine + step, n_peer)
        return other, lax.div(other, n_probe), lax.rem(other, n_probe)

    def sister(step):
        other = lax.rem(group + step, n_group)
        return other, 2 * other + side

    barrier = pltpu.get_barrier_semaphore()
    for step in range(1, n_peer):
        _, px, pp = peer(step)
        pl.semaphore_signal(barrier, inc=1, device_id=(base + px, pp), device_id_type=MESH)
    for step in range(1, n_group):
        pl.semaphore_signal(
            barrier, inc=1, device_id=(sister(step)[1], probe), device_id_type=MESH
        )
    pl.semaphore_wait(barrier, n_peer + n_group - 2)

    def remote(src, dst, send, recv, dev):
        return pltpu.make_async_remote_copy(
            src_ref=src, dst_ref=dst, send_sem=send, recv_sem=recv,
            device_id=dev, device_id_type=MESH,
        )

    own_plane = 2 + 2 * side
    got_plane = 4 - 2 * side

    band_at = pl.ds(probe * band, band)
    own_f = pltpu.make_async_copy(fields_ref, field.at[pl.ds(1 + 2 * side, 2)], f_own)
    own_f.start()
    x_f = remote(
        fields_ref.at[:, :, band_at], field.at[pl.ds(1 + 2 * side, 2), :, band_at],
        f_xs, f_xr, (partner, probe),
    )
    x_f.start()

    def z_low(src, plane, send):
        return remote(
            src.at[plane, pl.ds(0, 4), band_at], field.at[5, pl.ds(0, 4), band_at],
            send, f_hir, (below, probe),
        )

    def z_high(src, plane, send):
        return remote(
            src.at[plane, pl.ds(0, 4), band_at], field.at[0, pl.ds(0, 4), band_at],
            send, f_lor, (above, probe),
        )

    def share_copy(kind, step):
        if kind == 0:
            ref = field.at[pl.ds(3 - 2 * side, 2), :, band_at]
        else:
            ref = field.at[0 if kind == 1 else 5, pl.ds(0, 4), band_at]
        to = lax.rem(probe + step, n_probe)
        return remote(
            ref, ref, s_send.at[kind, step], s_recv.at[kind, n_probe - step], (space, to)
        )

    def share_start(kind):
        for step in range(1, n_probe):
            share_copy(kind, step).start()

    def share_wait(kind):
        for step in range(1, n_probe):
            share_copy(kind, step).wait_recv()

    def share_drain(kind):
        for step in range(1, n_probe):
            share_copy(kind, step).wait_send()

    direct_lo = (side == 0) & has_lo
    direct_hi = (side == 1) & has_hi
    relay_hi = (side == 0) & has_hi
    relay_lo = (side == 1) & has_lo

    @pl.when(direct_lo)
    def _():
        z_low(fields_ref, 0, f_zds).start()

    @pl.when(direct_hi)
    def _():
        z_high(fields_ref, 1, f_zds).start()

    def chunk_at(c):
        return pl.ds(c * per, per)

    def x_copy(c):
        return remote(
            probes_ref.at[pl.ds((1 - side) * half + c * per, per)],
            fwd_state.at[chunk_at(c), pl.ds(own_plane, 2)],
            x_send.at[c], x_recv.at[c], (partner, probe),
        )

    def own_copy(c):
        return pltpu.make_async_copy(
            probes_ref.at[pl.ds(side * half + c * per, per)],
            fwd_state.at[chunk_at(c), pl.ds(own_plane, 2)],
            own_sem.at[c],
        )

    def zd_src(c):
        return probes_ref.at[pl.ds(side * half + c * per, per)]

    def zf_src(c):
        return fwd_state.at[chunk_at(c), pl.ds(got_plane, 2)]

    def lo_copy(src, c, send):
        return remote(
            src, fwd_state.at[chunk_at(c), pl.ds(6, 2)], send.at[c], hi_recv.at[c], (below, probe)
        )

    def hi_copy(src, c, send):
        return remote(
            src, fwd_state.at[chunk_at(c), pl.ds(0, 2)], send.at[c], lo_recv.at[c], (above, probe)
        )

    def launch(c):
        x_copy(c).start()
        own_copy(c).start()

        @pl.when(direct_lo)
        def _():
            lo_copy(zd_src(c), c, zd_send).start()

        @pl.when(direct_hi)
        def _():
            hi_copy(zd_src(c), c, zd_send).start()

    for c in range(window):
        launch(c)

    @pl.when(jnp.logical_not(has_lo))
    def _():
        field[0] = jnp.zeros(field.shape[1:], jnp.float32)

        def clear(i, carry):
            fwd_state[i, pl.ds(0, 2)] = jnp.zeros((2, ny, nz), jnp.float32)
            return carry

        lax.fori_loop(0, half, clear, 0)

    @pl.when(jnp.logical_not(has_hi))
    def _():
        field[5] = jnp.zeros(field.shape[1:], jnp.float32)

        def clear(i, carry):
            fwd_state[i, pl.ds(6, 2)] = jnp.zeros((2, ny, nz), jnp.float32)
            return carry

        lax.fori_loop(0, half, clear, 0)

    x_f.wait_recv()

    @pl.when(relay_hi)
    def _():
        z_high(field, 4, f_zfs).start()

    @pl.when(relay_lo)
    def _():
        z_low(field, 1, f_zfs).start()

    share_start(0)

    @pl.when(has_lo)
    def _():
        z_high(field, 0, f_zfs).wait_recv()
        share_start(1)

    @pl.when(has_hi)
    def _():
        z_low(field, 5, f_zfs).wait_recv()
        share_start(2)

    own_f.wait()
    share_wait(0)

    @pl.when(has_lo)
    def _():
        share_wait(1)

    @pl.when(has_hi)
    def _():
        share_wait(2)

    row_id = lax.broadcasted_iota(jnp.int32, (ny, nz), 0)
    col_id = lax.broadcasted_iota(jnp.int32, (ny, nz), 1)

    def make_coef(plane, carry):
        centre = jnp.full((ny, nz), 1.0 - 6.0 * diffusion, jnp.float32)
        for dim in range(3):
            speed = field[plane, dim]
            pos, neg = jnp.maximum(speed, 0.0), jnp.minimum(speed, 0.0)
            centre = centre - pos + neg
            up, down = pos + diffusion, diffusion - neg
            if dim == 1:
                up = jnp.where(row_id == 0, 0.0, up)
                down = jnp.where(row_id == ny - 1, 0.0, down)
            if dim == 2:
                up = jnp.where(col_id == 0, 0.0, up)
                down = jnp.where(col_id == nz - 1, 0.0, down)
            coef[plane, 1 + 2 * dim] = up
            coef[plane, 2 + 2 * dim] = down
        coef[plane, 0] = centre
        return carry

    lax.fori_loop(0, 6, make_coef, 0)

    def one_probe(i, carry):
        def tangent(plane, inner):
            u = fwd_state[i, plane + 1]
            out = coef[plane, 0] * u
            out += coef[plane, 1] * fwd_state[i, plane]
            out += coef[plane, 2] * fwd_state[i, plane + 2]
            out += coef[plane, 3] * pltpu.roll(u, 1, 0)
            out += coef[plane, 4] * pltpu.roll(u, ny - 1, 0)
            out += coef[plane, 5] * pltpu.roll(u, 1, 1)
            out += coef[plane, 6] * pltpu.roll(u, nz - 1, 1)
            weighted[plane] = field[plane, 3] * out
            return inner

        lax.fori_loop(0, 6, tangent, 0)

        def adjoint(at, inner):
            plane = at + 1
            v = weighted[plane]
            out = coef[plane, 0] * v + field[plane, 4] * fwd_state[i, plane + 1]
            out += coef[plane + 1, 1] * weighted[plane + 1]
            out += coef[plane - 1, 2] * weighted[plane - 1]
            out += pltpu.roll(coef[plane, 3] * v, ny - 1, 0)
            out += pltpu.roll(coef[plane, 4] * v, 1, 0)
            out += pltpu.roll(coef[plane, 5] * v, nz - 1, 1)
            out += pltpu.roll(coef[plane, 6] * v, 1, 1)
            image[i, at] = out
            return inner

        lax.fori_loop(0, 4, adjoint, 0)
        return carry

    def block_src(first, count, px, pp):
        return image.at[pl.ds(first, count), pl.ds(2 * px, 2), pl.ds(pp * band, band)]

    def block_dst(owner, first, count):
        return rows_ref.at[pl.ds(owner * half + first, count)]

    def rank_of(px, pp):
        return pp * 2 + px

    my_rank = rank_of(side, probe)

    def step_body(c, carry):
        @pl.when(c < chunks)
        def _():
            x_copy(c).wait_recv()

            @pl.when(relay_hi)
            def _():
                hi_copy(zf_src(c), c, zf_send).start()

            @pl.when(relay_lo)
            def _():
                lo_copy(zf_src(c), c, zf_send).start()

            @pl.when(c + window < chunks)
            def _():
                launch(c + window)

        @pl.when(c > 0)
        def _():
            d = c - 1
            own_copy(d).wait()

            @pl.when(has_lo)
            def _():
                hi_copy(zf_src(d), d, zf_send).wait_recv()

            @pl.when(has_hi)
            def _():
                lo_copy(zf_src(d), d, zf_send).wait_recv()

            lax.fori_loop(d * per, (d + 1) * per, one_probe, 0)
            for step in range(1, n_peer):
                _, px, pp = peer(step)
                remote(
                    block_src(d * per, per, px, pp), block_dst(my_rank, d * per, per),
                    a_send.at[step], a_recv.at[n_peer - step], (base + px, pp),
                ).start()
            pltpu.make_async_copy(
                block_src(d * per, per, side, probe), block_dst(my_rank, d * per, per), a_own
            ).start()

        return carry

    lax.fori_loop(0, chunks + 1, step_body, 0)

    for step in range(1, n_peer):
        _, px, pp = peer(step)
        remote(
            block_src(0, half, px, pp), block_dst(rank_of(px, pp), 0, half),
            a_send.at[step], a_recv.at[step], (base + px, pp),
        ).wait()
    pltpu.make_async_copy(
        block_src(0, half, side, probe), block_dst(my_rank, 0, half), a_own
    ).wait()

    y_copy = pltpu.make_async_copy(rows_ref, y_out, y_sem)
    y_copy.start()

    count = rows_ref.shape[0]
    depth = rows_ref.shape[1] * band
    flat = rows_ref.reshape(count * depth, nz)
    gram_acc[...] = jnp.zeros_like(gram_acc)

    def gram_step(t, carry):
        cols = jnp.concatenate(
            [flat[pl.ds(t * 8 + r, count, stride=depth), :] for r in range(8)], axis=1
        )
        both = jnp.concatenate(split(cols), axis=0)
        gram_acc[...] += lax.dot_general(
            both, both, (((1,), (1,)), ((), ())), preferred_element_type=jnp.float32
        )
        return carry

    lax.fori_loop(0, depth // 8, gram_step, 0, unroll=2)
    across = gram_acc[:count, count:] + gram_acc[count:, :count]
    gram_part[...] = gram_acc[:count, :count] + (across + gram_acc[count:, count:])

    share = count // n_peer

    def r_copy(step):
        other, px, pp = peer(step)
        return remote(
            gram_part.at[pl.ds(other * share, share)], reduce_buf.at[mine],
            r_send.at[step], r_recv.at[n_peer - step], (base + px, pp),
        )

    for step in range(1, n_peer):
        r_copy(step).start()
    reduce_buf[mine] = gram_part[pl.ds(pl.multiple_of(mine * share, share), share)]
    for step in range(1, n_peer):
        r_copy(step).wait_recv()
    group_buf[group] = jnp.sum(reduce_buf[...], axis=0)

    def g_copy(step):
        other, at = sister(step)
        return remote(
            group_buf.at[group], group_buf.at[group],
            g_send.at[step], g_recv.at[n_group - step], (at, probe),
        )

    for step in range(1, n_group):
        g_copy(step).start()
    for step in range(1, n_group):
        g_copy(step).wait_recv()
    total[pl.ds(pl.multiple_of(mine * share, share), share)] = jnp.sum(group_buf[...], axis=0)

    def t_copy(step):
        _, px, pp = peer(step)
        return remote(
            total.at[pl.ds(mine * share, share)], total.at[pl.ds(mine * share, share)],
            t_send.at[step], t_recv.at[n_peer - step], (base + px, pp),
        )

    for step in range(1, n_peer):
        t_copy(step).start()
    for step in range(1, n_peer):
        t_copy(step).wait_recv()
    gram_out[...] = total[...]

    for step in range(1, n_peer):
        r_copy(step).wait_send()
        t_copy(step).wait_send()
    for step in range(1, n_group):
        g_copy(step).wait_send()
    x_f.wait_send()
    share_drain(0)

    @pl.when(has_lo)
    def _():
        share_drain(1)

    @pl.when(has_hi)
    def _():
        share_drain(2)

    @pl.when(direct_lo)
    def _():
        z_low(fields_ref, 0, f_zds).wait_send()

    @pl.when(direct_hi)
    def _():
        z_high(fields_ref, 1, f_zds).wait_send()

    @pl.when(relay_hi)
    def _():
        z_high(field, 4, f_zfs).wait_send()

    @pl.when(relay_lo)
    def _():
        z_low(field, 1, f_zfs).wait_send()

    def drain(c, carry):
        x_copy(c).wait_send()

        @pl.when(direct_lo)
        def _():
            lo_copy(zd_src(c), c, zd_send).wait_send()

        @pl.when(direct_hi)
        def _():
            hi_copy(zd_src(c), c, zd_send).wait_send()

        @pl.when(relay_hi)
        def _():
            hi_copy(zf_src(c), c, zf_send).wait_send()

        @pl.when(relay_lo)
        def _():
            lo_copy(zf_src(c), c, zf_send).wait_send()

        return carry

    lax.fori_loop(0, chunks, drain, 0)
    y_copy.wait()


def exchange(probes, fields, n_space, n_probe, chunks=4, window=4):
    local, planes, ny, nz = probes.shape
    count = local * n_probe
    half = local // 2
    band = ny // n_probe
    n_peer, n_group = 2 * n_probe, n_space // 2
    share = count // n_peer
    f32 = jnp.float32
    dma = pltpu.SemaphoreType.DMA
    return pl.pallas_call(
        functools.partial(exchange_kernel, n_space, n_probe, chunks, window),
        out_shape=(
            jax.ShapeDtypeStruct((count, planes, band, nz), f32),
            jax.ShapeDtypeStruct((count, count), f32),
        ),
        in_specs=[pl.BlockSpec(memory_space=pl.ANY)] * 2,
        out_specs=(
            pl.BlockSpec(memory_space=pl.ANY),
            pl.BlockSpec(memory_space=pltpu.VMEM),
        ),
        scratch_shapes=[
            pltpu.VMEM((6, 5, ny, nz), f32),
            pltpu.VMEM((half, 8, ny, nz), f32),
            pltpu.VMEM((6, 7, ny, nz), f32),
            pltpu.VMEM((6, ny, nz), f32),
            pltpu.VMEM((half, 4, ny, nz), f32),
            pltpu.VMEM((count, planes, band, nz), f32),
            pltpu.VMEM((2 * count, 2 * count), f32),
            pltpu.VMEM((count, count), f32),
            pltpu.VMEM((n_peer, share, count), f32),
            pltpu.VMEM((n_group, share, count), f32),
            pltpu.VMEM((count, count), f32),
        ]
        + [dma((chunks,))] * 7
        + [dma(())] * 7
        + [dma((3, n_probe))] * 2
        + [dma((n_peer,)), dma((n_peer,)), dma(())]
        + [dma((n_peer,)), dma((n_peer,)), dma((n_group,)), dma((n_group,))]
        + [dma((n_peer,)), dma((n_peer,)), dma(())],
        compiler_params=pltpu.CompilerParams(
            collective_id=0, has_side_effects=True, vmem_limit_bytes=48 * 1024 * 1024
        ),
        name="exchange",
    )(probes, fields)


def split(values):
    high = values.astype(jnp.bfloat16)
    low = (values - high.astype(jnp.float32)).astype(jnp.bfloat16)
    return high, low


def terms(values):
    found = []
    for _ in range(3):
        found.append(values.astype(jnp.bfloat16).astype(jnp.float32))
        values = values - found[-1]
    return found


def factor(gram_ref, work, n, rows=8):
    work[:, :n] = gram_ref[...]
    row_id = lax.broadcasted_iota(jnp.int32, (n, n), 0)
    col_id = lax.broadcasted_iota(jnp.int32, (n, n), 1)
    work[:, n:] = jnp.where(row_id == col_id, 1.0, 0.0)
    sub = lax.broadcasted_iota(jnp.int32, (rows, n), 0)
    lane = lax.broadcasted_iota(jnp.int32, (rows, n), 1)

    def panel_step(at, carry):
        start = pl.multiple_of(at * rows, rows)
        left = pltpu.roll(work[pl.ds(start, rows), :n], lax.rem(n - start, n), 1)
        right = work[pl.ds(start, rows), n:]
        columns = [jnp.broadcast_to(left[:, j : j + 1], (rows, n)) for j in range(rows)]
        pivots = columns[0]
        for j in range(rows):
            pivot = jnp.broadcast_to(columns[j][j : j + 1, :], (rows, n))
            times = jnp.where(sub > j, columns[j] * (1.0 / pivot), 0.0)
            pivots = jnp.where(sub == j, pivot, pivots)
            if j == rows - 1:
                break
            for i in range(j + 1, rows):
                columns[i] -= times * jnp.broadcast_to(columns[i][j : j + 1, :], (rows, n))
            left -= times * jnp.broadcast_to(left[j : j + 1, :], (rows, n))
            right -= times * jnp.broadcast_to(right[j : j + 1, :], (rows, n))
        scale = lax.rsqrt(pivots)
        scale = scale * (1.5 - 0.5 * (pivots * scale) * scale)
        left = pltpu.roll(left * scale, start, 1)
        right = right * scale
        ahead = jnp.where(lane >= start + rows, left, 0.0)
        both = jnp.concatenate([left, right], axis=1)
        a_terms, b_terms = terms(ahead), terms(both)
        pairs = ((0, 0), (0, 1), (1, 0), (1, 1), (0, 2), (2, 0))
        stacked_a = jnp.concatenate([a_terms[i] for i, _ in pairs], axis=0)
        stacked_b = jnp.concatenate([b_terms[i] for _, i in pairs], axis=0)
        work[...] -= lax.dot_general(
            stacked_a.astype(jnp.bfloat16), stacked_b.astype(jnp.bfloat16),
            (((0,), (0,)), ((), ())), preferred_element_type=jnp.float32,
        )
        work[pl.ds(start, rows), :] = both
        return carry

    lax.fori_loop(0, n // rows, panel_step, 0)
    upper = jnp.where(row_id <= col_id, work[:, :n], 0.0)
    return upper, work[:, n:]


def basis_kernel(
    norm_scale, gram_ref, y_ref, out_hbm, factor_ref, work, out_ref, out_sem
):
    count, depth, nz = y_ref.shape
    upper, inverse = factor(gram_ref, work, count)
    factor_ref[...] = upper / norm_scale
    high, low = split(inverse * norm_scale)
    left = jnp.concatenate([high, low, high, low], axis=1)
    flat = y_ref.reshape(count * depth, nz)
    result_flat = out_ref.reshape(count * depth, nz)
    rows = 8

    def store(t):
        part = pl.ds(pl.multiple_of(t * rows, rows), rows)
        return pltpu.make_async_copy(out_ref.at[:, part], out_hbm.at[:, part], out_sem.at[t])

    def block_step(t, carry):
        cols = jnp.concatenate(
            [flat[pl.ds(t * rows + r, count, stride=depth), :] for r in range(rows)], axis=1
        )
        y_high, y_low = split(cols)
        right = jnp.concatenate([y_high, y_high, y_low, y_low], axis=0)
        result = jnp.dot(left, right, preferred_element_type=jnp.float32)
        for r in range(rows):
            result_flat[pl.ds(t * rows + r, count, stride=depth), :] = result[
                :, r * nz : (r + 1) * nz
            ]
        store(t).start()
        return carry

    lax.fori_loop(0, depth // rows, block_step, 0, unroll=2)

    def drain(t, carry):
        store(t).wait()
        return carry

    lax.fori_loop(0, depth // rows, drain, 0)


def basis(gram_matrix, y_rows, norm_scale):
    count, depth, nz = y_rows.shape
    f32 = jnp.float32
    vmem = pl.BlockSpec(memory_space=pltpu.VMEM)
    hbm = pl.BlockSpec(memory_space=pl.ANY)
    return pl.pallas_call(
        functools.partial(basis_kernel, norm_scale),
        out_shape=(
            jax.ShapeDtypeStruct(y_rows.shape, f32),
            jax.ShapeDtypeStruct(gram_matrix.shape, f32),
        ),
        in_specs=[vmem, vmem],
        out_specs=(hbm, vmem),
        scratch_shapes=[
            pltpu.VMEM((count, 2 * count), f32),
            pltpu.VMEM(y_rows.shape, f32),
            pltpu.SemaphoreType.DMA((depth // 8,)),
        ],
        compiler_params=pltpu.CompilerParams(vmem_limit_bytes=24 * 1024 * 1024),
        name="basis",
    )(gram_matrix, y_rows)


def per_device(probes, winds, wind_step, obs_weight, prior_weight):
    n_space, n_probe = lax.axis_size("space"), lax.axis_size("probe")
    wind_now = select_wind(winds, wind_step)
    fields = jnp.concatenate([wind_now, obs_weight[None], prior_weight[None]], axis=0)
    fields = jnp.swapaxes(fields, 0, 1)
    image, gram_matrix = exchange(probes, fields, n_space, n_probe)
    count, planes, band, nz = image.shape
    norm_scale = math.sqrt(planes * band * nz * n_space * n_probe)
    basis_out, r_factor = basis(
        gram_matrix, image.reshape(count, planes * band, nz), norm_scale
    )
    return (basis_out.reshape(image.shape), r_factor)


def solution(mesh):
    placed = (
        P("probe", "space", None, None),
        P(None, None, "space", None, None),
        P("space"),
        P("space", None, None),
        P("space", None, None),
    )
    return jax.shard_map(
        per_device,
        mesh=mesh,
        in_specs=placed,
        out_specs=(P(None, "space", "probe", None), P()),
        check_vma=False,
    )
```
